32 devices in a mesh: tm: 4 (over y, x), space: 8 (over z, core).
Axes of the slice: x: 2, y: 2, z: 4, core: 2. Of those that a mesh axis runs over, the one named last changes fastest.
Arguments:
- iterate: float32 [64, 5, 16384], P('tm', None, 'space'), may hold values from -6 to 6
- right_side: float32 [64, 5, 16384], P('tm', None, 'space'), may hold values from -6 to 6
- jacobian: float32 [6, 5, 5, 16384], P(None, None, None, 'space'), may hold values from -0.24 to 0.24
- self_block: float32 [5, 5, 16384], P(None, None, 'space'), may hold values from -0.48 to 0.48
- cell_diag: float32 [5, 16384], P(None, 'space'), may hold values from 2.5 to 5
- neighbours: int32 [128, 6], P('space'), may hold values from 0 to 31, as said below
- face_list: int32 [64], P('space'), may hold values from 0 to 15, as said below
Outputs:
- updated: float32 [64, 5, 16384], P('tm', None, 'space')
- residual: float32 [64, 5, 16384], P('tm', None, 'space')
The draws below stay inside these ranges and needn't reach their ends.
Inputs may be any that keep to these rules, and one draw needn't show every extreme that they name: `neighbours`: row b of slab s names 6 blocks in slab s's extended numbering: 0 to 15 its own blocks, 16 + h the h-th face block of slab s-1, 24 + h the h-th face block of slab s+1. Entry 0 always names a face block of the lower slab, entry 1 one of the upper slab, entries 2 to 5 own blocks. `face_list`: each slab's 8 entries are distinct local blocks of that slab; the last entry is always the slab's last block.
All inputs are finite; a program needn't handle non-finite values.
Results may differ from the reference program's by a relative error of at most 0.0001.
Values sent between devices are 32-bit elements; how exact they have to be, the bound alone decides.
No kernel may reach another device: no remote copies, remote signals or barrier semaphores. Data moves between devices by JAX's collectives and lax.ppermute only.
A program may use at most 64 MiB of HBM per device.

```python
import math
import jax
import jax.numpy as jnp

NV = 5
BLK = 128
K = 6
NT = 64
NU1 = 2
NU2 = 2
NUC = 4
BD = 16
H = 8
NTC = 16
NB = 128
NC = 16384
FACES = 64
N_SPACE = 8


def draw_neighbours(key, part):
    shard_count = NB // BD
    keys = jax.random.split(key, 4)
    lower_shift = jax.random.randint(keys[0], (shard_count, 1), 0, H)
    upper_shift = jax.random.randint(keys[1], (shard_count, 1), 0, H)
    local = jnp.arange(BD, dtype=jnp.int32)[None, :]
    first = BD + (local + lower_shift) % H
    second = BD + H + (BD - 1 - local + upper_shift) % H
    third = jax.vmap(lambda sub_key: jax.random.permutation(sub_key, BD))(jax.random.split(keys[2], shard_count))
    others = jax.random.randint(keys[3], (shard_count, BD, K - 3), 0, BD)
    table = jnp.concatenate([first[:, :, None].astype(jnp.int32), second[:, :, None].astype(jnp.int32), third[:, :, None].astype(jnp.int32), others.astype(jnp.int32)], axis=2)
    return table.reshape(NB, K).astype(jnp.int32)


def draw_face_list(key, part):
    shard_count = FACES // H

    def one_slab(sub_key):
        chosen = jax.random.permutation(sub_key, BD - 1)[:H - 1].astype(jnp.int32)
        return jnp.concatenate([chosen, jnp.full((1,), BD - 1, jnp.int32)])
    return jax.vmap(one_slab)(jax.random.split(key, shard_count)).reshape(FACES).astype(jnp.int32)


def block_scale(rng, dims, shards, smallest, largest):
    gain = 1.0
    for dim, shards_of in shards:
        draws = jax.random.uniform(jax.random.fold_in(jax.random.fold_in(rng, 6), dim), (shards_of,), jnp.float32, smallest / len(shards), largest / len(shards))
        gain = gain * jnp.repeat(jnp.exp(draws), dims[dim] // shards_of).reshape((-1,) + (1,) * (len(dims) - 1 - dim))
    return gain


def noise(key, shape, spread, limit, cuts=(), kind=jnp.bfloat16):
    level = block_scale(key, shape, cuts, -0.22, 0.18) if cuts else 1.0
    array = jax.random.normal(key, shape, jnp.float32) * spread * level
    return jnp.minimum(jnp.maximum(array, -limit), limit).astype(kind)


def setup_inputs(seed: int = 0) -> dict:
    arg_keys = jax.random.split(jax.random.key(seed), 8)
    return {
        "iterate": noise(arg_keys[0], (NT, NV, NC), 1.0, 6.0, ((0, 4), (2, 8)), jnp.float32),
        "right_side": noise(arg_keys[1], (NT, NV, NC), 1.0, 6.0, ((0, 4), (2, 8)), jnp.float32),
        "jacobian": noise(arg_keys[2], (K, NV, NV, NC), 0.04, 0.24, ((3, 8),), jnp.float32),
        "self_block": noise(arg_keys[3], (NV, NV, NC), 0.08, 0.48, ((2, 8),), jnp.float32),
        "cell_diag": jnp.clip(jnp.exp(math.log(5.0) - 0.6931472 * jax.random.uniform(arg_keys[4], (NV, NC), jnp.float32) ** block_scale(arg_keys[4], (NV, NC), ((1, 8),), -0.2, 0.2)), 2.5, 5.0),
        "neighbours": draw_neighbours(jax.random.fold_in(arg_keys[7], 71), 0),
        "face_list": draw_face_list(jax.random.fold_in(arg_keys[7], 71), 0),
    }


time_weight = 0.5
damping = 0.7


def pick_blocks(blocks, block_index):
    return jax.vmap(lambda part_blocks, chosen: jnp.take(part_blocks, chosen, axis=2), in_axes=(2, 0), out_axes=2)(blocks, block_index)


def space_term(field, jacobian, self_block, cell_diag, neighbours, face_list):
    step_count = field.shape[0]
    blocks = field.reshape(step_count, NV, N_SPACE, BD, BLK)
    outgoing = pick_blocks(blocks, face_list.reshape(N_SPACE, H))
    empty = jnp.zeros_like(outgoing[:, :, :1])
    lower_rim = jnp.concatenate([empty, outgoing[:, :, :-1]], axis=2)
    upper_rim = jnp.concatenate([outgoing[:, :, 1:], empty], axis=2)
    extended = jnp.concatenate([blocks, lower_rim, upper_rim], axis=3)
    slot_table = neighbours.reshape(N_SPACE, BD, K)
    off_diag = self_block * (1.0 - jnp.eye(NV, dtype=jnp.float32))[:, :, None]
    summed = jnp.sum(off_diag[None] * field[:, None], axis=2) + cell_diag[None] * field
    for neighbour_slot in range(K):
        picked = pick_blocks(extended, slot_table[:, :, neighbour_slot]).reshape(step_count, NV, N_SPACE * BD * BLK)
        summed = summed + jnp.sum(jacobian[neighbour_slot][None] * picked[:, None], axis=2)
    return summed


def operator(field, weight, jacobian, self_block, cell_diag, neighbours, face_list):
    back_one = jnp.roll(field, 1, axis=0)
    back_two = jnp.roll(field, 2, axis=0)
    timed = weight * (3.0 * field - 4.0 * back_one + back_two)
    return timed + space_term(field, jacobian, self_block, cell_diag, neighbours, face_list)


def reference(iterate, right_side, jacobian, self_block, cell_diag, neighbours, face_list):
    extra = (jacobian, self_block, cell_diag, neighbours, face_list)
    inverse_fine = 1.0 / (3.0 * time_weight + cell_diag)
    coarse_weight = time_weight / 4.0
    inverse_coarse = 1.0 / (3.0 * coarse_weight + cell_diag)
    state = iterate
    for sweep_no in range(NU1):
        state = state + damping * inverse_fine * (right_side - operator(state, time_weight, *extra))
    defect = right_side - operator(state, time_weight, *extra)
    coarse_defect = defect.reshape(NTC, 4, NV, NC).mean(axis=1)
    correction = damping * inverse_coarse * coarse_defect
    for sweep_no in range(NUC - 1):
        correction = correction + damping * inverse_coarse * (coarse_defect - operator(correction, coarse_weight, *extra))
    state = state + jnp.repeat(correction, 4, axis=0)
    for sweep_no in range(NU2):
        state = state + damping * inverse_fine * (right_side - operator(state, time_weight, *extra))
    residual = right_side - operator(state, time_weight, *extra)
    return state, residual
```

```python
import functools

import jax
import jax.numpy as jnp
from jax import lax
from jax.experimental import pallas as pl
from jax.experimental.pallas import tpu as pltpu
from jax.sharding import PartitionSpec as P

NV = 5
BLK = 128
K = 6
NU1 = 2
NU2 = 2
NUC = 4
GROUP = 4

time_weight = 0.5
coarse_weight = time_weight / GROUP
damping = 0.7

SCRATCH_BYTES = 4 << 20
IN_VMEM = pl.BlockSpec(memory_space=pltpu.VMEM)
IN_SMEM = pl.BlockSpec(memory_space=pltpu.SMEM)


def call(kernel, name, tables, arrays, outs, flops=0):
    arrays = [pltpu.with_memory_space_constraint(a, pltpu.VMEM) for a in arrays]
    tables = [pltpu.with_memory_space_constraint(t, pltpu.SMEM) for t in tables]
    size = sum(a.size * 4 for a in arrays) + sum(4 * o.size for o in outs)
    return pl.pallas_call(
        kernel,
        out_shape=[pltpu.VMEM(o.shape, jnp.float32) for o in outs],
        in_specs=[IN_SMEM] * len(tables) + [IN_VMEM] * len(arrays),
        out_specs=[IN_VMEM] * len(outs),
        cost_estimate=pl.CostEstimate(flops=flops, bytes_accessed=size, transcendentals=0),
        compiler_params=pltpu.CompilerParams(vmem_limit_bytes=SCRATCH_BYTES),
        name=name,
    )(*tables, *arrays)


def shape(*dims):
    return jax.ShapeDtypeStruct(dims, jnp.float32)


def lanes_of(b):
    return pl.ds(pl.multiple_of(b * BLK, BLK), BLK)


def cross_slot():
    return lax.rem(lax.axis_index("space"), 2)


def coupled(total, jacobian, slot, lanes, values):
    for j in range(NV):
        for a in range(NV):
            total[a] = total[a] - jacobian[slot, a, pl.ds(j, 1), lanes] * values[j]
    return total


def earlier(v, steps):
    if v.shape[0] <= steps:
        return jnp.zeros_like(v)
    return jnp.concatenate([jnp.zeros((steps, BLK), jnp.float32), v[: v.shape[0] - steps]], axis=0)


def each_block(count, step):
    lax.fori_loop(0, count, lambda b, c: (step(b), c)[1], 0)


def own_part(total, b, field, rim, tables, jacobian, self_block, faces):
    lanes = lanes_of(b)
    v = [field[b, j] for j in range(NV)]
    for a in range(NV):
        for j in range(NV):
            if j != a:
                total[a] = total[a] - self_block[a, pl.ds(j, 1), lanes] * v[j]
    for slot in range(2, K):
        block = tables[b, slot]
        total = coupled(total, jacobian, slot, lanes, [field[block, j] for j in range(NV)])
    slot = 1 - cross_slot()
    block = tables[b, slot] - (field.shape[0] + faces * slot)
    return coupled(total, jacobian, slot, lanes, [rim[block, j] for j in range(NV)])


def cross_part(total, b, blocks, rim, tables, jacobian, faces):
    slot = cross_slot()
    block = tables[b, slot] - (blocks + faces * slot)
    return coupled(total, jacobian, slot, lanes_of(b), [rim[block, j] for j in range(NV)])


def tail_rows(v, weight):
    steps = v.shape[0]
    last = v[steps - 1 :]
    return weight * jnp.concatenate([v[steps - 2 : steps - 1] - 4.0 * last, last], axis=0)


def send_faces(faces_out, field, face_list):
    for h in range(faces_out.shape[0]):
        for a in range(NV):
            faces_out[h, a] = field[face_list[h], a]


def send_tail(tail_out, field, weight):
    def step(b):
        for a in range(NV):
            tail_out[b, a] = tail_rows(field[b, a], weight)

    each_block(tail_out.shape[0], step)


def inverse_rows(cell_diag, a, lanes, weight):
    return damping / (3.0 * weight + cell_diag[pl.ds(a, 1), lanes])


def first_faces(face_list, field, faces_out, tail_out):
    send_faces(faces_out, field, face_list)
    send_tail(tail_out, field, time_weight)


def own_kernel(weight, faces, tables, field, goal, rim, jacobian, self_block, cell_diag, out):
    def step(b):
        lanes = lanes_of(b)
        total = []
        for a in range(NV):
            v = field[b, a]
            point = 3.0 * weight + cell_diag[pl.ds(a, 1), lanes]
            timed = weight * (earlier(v, 2) - 4.0 * earlier(v, 1))
            total.append(goal[b, a] - point * v - timed)
        total = own_part(total, b, field, rim, tables, jacobian, self_block, faces)
        for a in range(NV):
            out[b, a] = total[a]

    each_block(field.shape[0], step)


def mean_kernel(weight, faces, tables, field, goal, means, rim, jacobian, self_block, cell_diag, out, scratch):
    steps = means.shape[2]

    def step(b):
        lanes = lanes_of(b)
        total = []
        for a in range(NV):
            v = field[b, a]
            scratch[...] = goal[b, a] - weight * (3.0 * v - 4.0 * earlier(v, 1) + earlier(v, 2))
            rows = sum(scratch[pl.ds(i, steps, stride=GROUP), :] for i in range(GROUP))
            total.append(rows * (1.0 / GROUP) - cell_diag[pl.ds(a, 1), lanes] * means[b, a])
        total = own_part(total, b, means, rim, tables, jacobian, self_block, faces)
        for a in range(NV):
            out[b, a] = total[a]

    each_block(field.shape[0], step)


def add_rows(total, rows):
    pad = total.shape[0] - rows.shape[0]
    if pad:
        rows = jnp.concatenate([rows, jnp.zeros((pad, BLK), jnp.float32)], axis=0)
    return total - rows


def sweep_kernel(weight, tables, face_list, field, part, rim, tail, jacobian, cell_diag, out, faces_out, tail_out):
    blocks, faces = field.shape[0], rim.shape[0]

    def step(b):
        total = [add_rows(part[b, a], tail[b, a]) for a in range(NV)]
        total = cross_part(total, b, blocks, rim, tables, jacobian, faces)
        for a in range(NV):
            v = field[b, a] + inverse_rows(cell_diag, a, lanes_of(b), weight) * total[a]
            out[b, a] = v
            tail_out[b, a] = tail_rows(v, weight)

    each_block(blocks, step)
    send_faces(faces_out, out, face_list)


def smoothed_kernel(
    weight, tables, face_list, field, part, rim, tail, jacobian, cell_diag, out, means_out, faces_out, tail_out
):
    blocks, faces, steps = field.shape[0], rim.shape[0], means_out.shape[2]

    def step(b):
        total = [add_rows(part[b, a], tail[b, a]) for a in range(NV)]
        total = cross_part(total, b, blocks, rim, tables, jacobian, faces)
        for a in range(NV):
            v = field[b, a] + inverse_rows(cell_diag, a, lanes_of(b), weight) * total[a]
            out[b, a] = v
            tail_out[b, a] = tail_rows(v, weight)
            rows = sum(out[b, a, pl.ds(i, steps, stride=GROUP), :] for i in range(GROUP))
            means_out[b, a] = rows * (1.0 / GROUP)

    each_block(blocks, step)
    send_faces(faces_out, means_out, face_list)


def first_correction_kernel(
    weight, tables, face_list, part, rim, tail, jacobian, cell_diag, defect_out, out, faces_out, tail_out
):
    blocks, faces = part.shape[0], rim.shape[0]

    def step(b):
        total = []
        for a in range(NV):
            rows = tail[b, a]
            rows = (rows[:1] + rows[1:]) * (1.0 / GROUP)
            total.append(add_rows(part[b, a], rows))
        total = cross_part(total, b, blocks, rim, tables, jacobian, faces)
        for a in range(NV):
            defect_out[b, a] = total[a]
            v = inverse_rows(cell_diag, a, lanes_of(b), weight) * total[a]
            out[b, a] = v
            tail_out[b, a] = tail_rows(v, weight)

    each_block(blocks, step)
    send_faces(faces_out, out, face_list)


def corrected_kernel(
    weight, tables, face_list, field, part, rim, tail, fine, jacobian, cell_diag, out, faces_out, tail_out
):
    blocks, faces, steps = field.shape[0], rim.shape[0], field.shape[2]

    def step(b):
        total = [add_rows(part[b, a], tail[b, a]) for a in range(NV)]
        total = cross_part(total, b, blocks, rim, tables, jacobian, faces)
        for a in range(NV):
            v = field[b, a] + inverse_rows(cell_diag, a, lanes_of(b), weight) * total[a]
            for i in range(GROUP):
                rows = pl.ds(i, steps, stride=GROUP)
                out[b, a, rows, :] = fine[b, a, rows, :] + v
            tail_out[b, a] = tail_rows(out[b, a], time_weight)

    each_block(blocks, step)
    send_faces(faces_out, out, face_list)


def residual_kernel(tables, part, rim, tail, jacobian, out):
    blocks, faces = part.shape[0], rim.shape[0]

    def step(b):
        total = [add_rows(part[b, a], tail[b, a]) for a in range(NV)]
        total = cross_part(total, b, blocks, rim, tables, jacobian, faces)
        for a in range(NV):
            out[b, a] = total[a]

    each_block(blocks, step)


def exchange(faces, tail):
    slabs, periods = lax.axis_size("space"), lax.axis_size("tm")
    across = [(i, i + 1) for i in range(1, slabs - 1, 2)]
    beside = [(i, i + 1) for i in range(0, slabs - 1, 2)]
    both_ways = lambda pairs: pairs + [(j, i) for i, j in pairs]
    rim_x = lax.ppermute(faces, "space", both_ways(across))
    rim_on = lax.ppermute(faces, "space", both_ways(beside))
    tail = lax.ppermute(tail, "tm", [(i, (i + 1) % periods) for i in range(periods)])
    return rim_x, rim_on, tail


def body(iterate, right_side, jacobian, self_block, cell_diag, neighbours, face_list):
    steps, cells = iterate.shape[0], iterate.shape[2]
    blocks, faces = cells // BLK, face_list.shape[0]
    coarse = steps // GROUP
    per_slot = 2 * blocks * NV * NV * BLK

    by_block = lambda x: jnp.transpose(x.reshape(steps, NV, blocks, BLK), (2, 1, 0, 3))
    by_step = lambda x: jnp.transpose(x, (2, 1, 0, 3)).reshape(steps, NV, cells)
    whole = lambda n: shape(blocks, NV, n, BLK)
    face = lambda n: shape(faces, NV, n, BLK)
    tail_shape = shape(blocks, NV, 2, BLK)

    state = by_block(iterate)
    goal = by_block(right_side)
    sent, tail = call(first_faces, "faces_of_iterate", [face_list], [state], [face(steps), tail_shape])

    def own(weight, n, field, target, rim_on):
        return call(
            functools.partial(own_kernel, weight, faces), "own_part", [neighbours],
            [field, target, rim_on, jacobian, self_block, cell_diag], [whole(n)], 6 * per_slot * n,
        )[0]

    def smooth(state, sent, tail):
        rim_x, rim_on, tail = exchange(sent, tail)
        part = own(time_weight, steps, state, goal, rim_on)
        return part, rim_x, tail

    for sweep_no in range(NU1):
        part, rim_x, tail = smooth(state, sent, tail)
        arrays = [state, part, rim_x, tail, jacobian, cell_diag]
        if sweep_no < NU1 - 1:
            state, sent, tail = call(
                functools.partial(sweep_kernel, time_weight), "sweep", [neighbours, face_list], arrays,
                [whole(steps), face(steps), tail_shape], per_slot * steps,
            )
        else:
            state, means, sent, tail = call(
                functools.partial(smoothed_kernel, time_weight), "sweep_and_means", [neighbours, face_list], arrays,
                [whole(steps), whole(coarse), face(coarse), tail_shape], per_slot * steps,
            )

    rim_x, rim_on, tail = exchange(sent, tail)
    scratch_kernel = functools.partial(mean_kernel, time_weight, faces)
    part = pl_mean(scratch_kernel, neighbours, [state, goal, means, rim_on, jacobian, self_block, cell_diag],
                   whole(coarse), steps, 6 * per_slot * coarse)
    defect, correction, sent, tail = call(
        functools.partial(first_correction_kernel, coarse_weight), "first_correction", [neighbours, face_list],
        [part, rim_x, tail, jacobian, cell_diag],
        [whole(coarse), whole(coarse), face(coarse), tail_shape], per_slot * coarse,
    )
    for sweep_no in range(NUC - 1):
        rim_x, rim_on, tail = exchange(sent, tail)
        part = own(coarse_weight, coarse, correction, defect, rim_on)
        if sweep_no < NUC - 2:
            correction, sent, tail = call(
                functools.partial(sweep_kernel, coarse_weight), "coarse_sweep", [neighbours, face_list],
                [correction, part, rim_x, tail, jacobian, cell_diag],
                [whole(coarse), face(coarse), tail_shape], per_slot * coarse,
            )
        else:
            state, sent, tail = call(
                functools.partial(corrected_kernel, coarse_weight), "corrected", [neighbours, face_list],
                [correction, part, rim_x, tail, state, jacobian, cell_diag],
                [whole(steps), face(steps), tail_shape], per_slot * coarse,
            )

    for sweep_no in range(NU2):
        part, rim_x, tail = smooth(state, sent, tail)
        state, sent, tail = call(
            functools.partial(sweep_kernel, time_weight), "sweep", [neighbours, face_list],
            [state, part, rim_x, tail, jacobian, cell_diag],
            [whole(steps), face(steps), tail_shape], per_slot * steps,
        )
    part, rim_x, tail = smooth(state, sent, tail)
    residual = call(
        residual_kernel, "residual", [neighbours], [part, rim_x, tail, jacobian], [whole(steps)], per_slot * steps
    )[0]
    return by_step(state), by_step(residual)


def pl_mean(kernel, neighbours, arrays, out, steps, flops):
    arrays = [pltpu.with_memory_space_constraint(a, pltpu.VMEM) for a in arrays]
    neighbours = pltpu.with_memory_space_constraint(neighbours, pltpu.SMEM)
    return pl.pallas_call(
        kernel,
        out_shape=pltpu.VMEM(out.shape, jnp.float32),
        in_specs=[IN_SMEM] + [IN_VMEM] * len(arrays),
        out_specs=IN_VMEM,
        scratch_shapes=[pltpu.VMEM((steps, BLK), jnp.float32)],
        cost_estimate=pl.CostEstimate(flops=flops, bytes_accessed=4 * out.size, transcendentals=0),
        compiler_params=pltpu.CompilerParams(vmem_limit_bytes=SCRATCH_BYTES),
        name="own_part_of_means",
    )(neighbours, *arrays)


def solution(mesh):
    in_specs = (
        P("tm", None, "space"),
        P("tm", None, "space"),
        P(None, None, None, "space"),
        P(None, None, "space"),
        P(None, "space"),
        P("space", None),
        P("space"),
    )
    out_specs = (P("tm", None, "space"), P("tm", None, "space"))
    return jax.shard_map(body, mesh=mesh, in_specs=in_specs, out_specs=out_specs, check_vma=False)
```

```python
import functools

import jax
import jax.numpy as jnp
from jax import lax
from jax.experimental import pallas as pl
from jax.experimental.pallas import tpu as pltpu
from jax.sharding import PartitionSpec as P

NV = 5
BLK = 128
K = 6
NU1 = 2
NU2 = 2
NUC = 4
GROUP = 4

time_weight = 0.5
coarse_weight = time_weight / GROUP
damping = 0.7

UNROLL = 2
SCRATCH_BYTES = 4 << 20
IN_VMEM = pl.BlockSpec(memory_space=pltpu.VMEM)
IN_SMEM = pl.BlockSpec(memory_space=pltpu.SMEM)


def call(kernel, name, tables, arrays, outs, flops=0, scratch=(), out_specs=None):
    arrays = [pltpu.with_memory_space_constraint(a, pltpu.VMEM) for a in arrays]
    size = 4 * (sum(a.size for a in arrays) + sum(o.size for o in outs))
    return pl.pallas_call(
        kernel,
        out_shape=outs if out_specs else [pltpu.VMEM(o.shape, o.dtype) for o in outs],
        in_specs=[IN_SMEM] * len(tables) + [IN_VMEM] * len(arrays),
        out_specs=out_specs or [IN_VMEM] * len(outs),
        scratch_shapes=scratch,
        cost_estimate=pl.CostEstimate(flops=flops, bytes_accessed=size, transcendentals=0),
        compiler_params=pltpu.CompilerParams(vmem_limit_bytes=SCRATCH_BYTES),
        name=name,
    )(*tables, *arrays)


def shape(*dims):
    return jax.ShapeDtypeStruct(dims, jnp.float32)


def lanes_of(b):
    return pl.ds(pl.multiple_of(b * BLK, BLK), BLK)


def cross_slot():
    return lax.rem(lax.axis_index("space"), 2)


def each_block(count, step):
    unroll = UNROLL if count % UNROLL == 0 else 1

    def steps(i, carry):
        for u in range(unroll):
            step(i * unroll + u, u)
        return carry

    lax.fori_loop(0, count // unroll, steps, 0)


def table_kernel(neighbours, face_list, table, listed):
    slot = cross_slot()
    slots, blocks = neighbours.shape
    faces = face_list.shape[0]

    def step(b, carry):
        table[0, b] = neighbours[slot, b] - (blocks + faces * slot)
        table[1, b] = neighbours[1 - slot, b] - (blocks + faces * (1 - slot))
        for k in range(2, slots):
            table[k, b] = neighbours[k, b]
        return carry

    lax.fori_loop(0, blocks, step, 0)
    for h in range(faces):
        listed[h] = face_list[h]


def points_kernel(cell_diag, fine_out, coarse_out):
    fine_out[...] = damping / (3.0 * time_weight + cell_diag[...])
    coarse_out[...] = damping / (3.0 * coarse_weight + cell_diag[...])


def rim_jacobian_kernel(jacobian, out):
    lower_crosses = cross_slot() == 0
    for a in range(NV):
        for j in range(NV):
            lower, upper = jacobian[a, j, pl.ds(0, 1), :], jacobian[a, j, pl.ds(1, 1), :]
            out[0, a, pl.ds(j, 1), :] = jnp.where(lower_crosses, lower, upper)
            out[1, a, pl.ds(j, 1), :] = jnp.where(lower_crosses, upper, lower)


def coupled(total, coupling, values):
    for j in range(NV):
        for a in range(NV):
            total[a] = total[a] - coupling(a, j) * values[j]
    return total


def earlier(v, steps):
    if v.shape[0] <= steps:
        return jnp.zeros_like(v)
    return jnp.concatenate([jnp.zeros((steps, BLK), jnp.float32), v[: v.shape[0] - steps]], axis=0)


def own_part(total, b, field, rim, table, jacobian, rim_jacobian, self_block):
    lanes = lanes_of(b)
    v = [field[j, :, lanes] for j in range(NV)]
    for a in range(NV):
        for j in range(NV):
            if j != a:
                total[a] = total[a] - self_block[a, pl.ds(j, 1), lanes] * v[j]
    for slot in range(2, K):
        there = lanes_of(table[slot, b])
        row = pl.ds(slot, 1)
        total = coupled(total, lambda a, j: jacobian[a, j, row, lanes], [field[j, :, there] for j in range(NV)])
    return rim_part(1, total, b, rim, table, rim_jacobian)


def rim_part(side, total, b, rim, table, rim_jacobian):
    block, lanes = table[side, b], lanes_of(b)
    coupling = lambda a, j: rim_jacobian[side, a, pl.ds(j, 1), lanes]
    return coupled(total, coupling, [rim[block, j] for j in range(NV)])


def faces_kernel(listed, field, faces_out):
    for h in range(faces_out.shape[0]):
        lanes = lanes_of(listed[h])
        for a in range(NV):
            faces_out[h, a] = field[a, :, lanes]


def tail_kernel(weight, field, tail_out):
    steps = field.shape[1]
    for a in range(NV):
        last = field[a, pl.ds(steps - 1, 1), :]
        tail_out[a, pl.ds(0, 1), :] = weight * (field[a, pl.ds(steps - 2, 1), :] - 4.0 * last)
        tail_out[a, pl.ds(1, 1), :] = weight * last


def own_kernel(weight, table, field, goal, rim, jacobian, rim_jacobian, self_block, cell_diag, out):
    def step(b, u):
        lanes = lanes_of(b)
        total = []
        for a in range(NV):
            v = field[a, :, lanes]
            point = 3.0 * weight + cell_diag[pl.ds(a, 1), lanes]
            timed = weight * (earlier(v, 2) - 4.0 * earlier(v, 1))
            total.append(goal[a, :, lanes] - point * v - timed)
        total = own_part(total, b, field, rim, table, jacobian, rim_jacobian, self_block)
        for a in range(NV):
            out[a, :, lanes] = total[a]

    each_block(table.shape[1], step)


def mean_rows(v, scratch, steps):
    scratch[...] = v
    return sum(scratch[pl.ds(i, steps, stride=GROUP), :] for i in range(GROUP)) * (1.0 / GROUP)


def means_kernel(weight, table, field, goal, means, rim, jacobian, rim_jacobian, self_block, cell_diag, out, scratch):
    steps = means.shape[1]

    def step(b, u):
        lanes = lanes_of(b)
        total = []
        for a in range(NV):
            v = field[a, :, lanes]
            fine = goal[a, :, lanes] - weight * (3.0 * v - 4.0 * earlier(v, 1) + earlier(v, 2))
            total.append(mean_rows(fine, scratch.at[u, a], steps) - cell_diag[pl.ds(a, 1), lanes] * means[a, :, lanes])
        total = own_part(total, b, means, rim, table, jacobian, rim_jacobian, self_block)
        for a in range(NV):
            out[a, :, lanes] = total[a]

    each_block(table.shape[1], step)


def less_rows(total, rows):
    pad = total.shape[0] - rows.shape[0]
    if pad:
        rows = jnp.concatenate([rows, jnp.zeros((pad, BLK), jnp.float32)], axis=0)
    return total - rows


def rest_part(b, part, rim, tail, table, rim_jacobian):
    lanes = lanes_of(b)
    total = [less_rows(part[a, :, lanes], tail[a, :, lanes]) for a in range(NV)]
    return rim_part(0, total, b, rim, table, rim_jacobian)


def sweep_kernel(table, listed, field, part, rim, tail, rim_jacobian, points, out, faces_out):
    def step(b, u):
        lanes = lanes_of(b)
        total = rest_part(b, part, rim, tail, table, rim_jacobian)
        for a in range(NV):
            out[a, :, lanes] = field[a, :, lanes] + points[pl.ds(a, 1), lanes] * total[a]

    each_block(table.shape[1], step)
    faces_kernel(listed, out, faces_out)


def smoothed_kernel(table, listed, field, part, rim, tail, rim_jacobian, points, out, means_out, faces_out, scratch):
    steps = means_out.shape[1]

    def step(b, u):
        lanes = lanes_of(b)
        total = rest_part(b, part, rim, tail, table, rim_jacobian)
        for a in range(NV):
            v = field[a, :, lanes] + points[pl.ds(a, 1), lanes] * total[a]
            out[a, :, lanes] = v
            means_out[a, :, lanes] = mean_rows(v, scratch.at[u, a], steps)

    each_block(table.shape[1], step)
    faces_kernel(listed, means_out, faces_out)


def first_correction_kernel(table, listed, part, rim, tail, rim_jacobian, points, defect_out, out, faces_out):
    def step(b, u):
        lanes = lanes_of(b)
        total = []
        for a in range(NV):
            rows = tail[a, :, lanes]
            total.append(less_rows(part[a, :, lanes], (rows[:1] + rows[1:]) * (1.0 / GROUP)))
        total = rim_part(0, total, b, rim, table, rim_jacobian)
        for a in range(NV):
            defect_out[a, :, lanes] = total[a]
            out[a, :, lanes] = points[pl.ds(a, 1), lanes] * total[a]

    each_block(table.shape[1], step)
    faces_kernel(listed, out, faces_out)


def corrected_kernel(table, listed, field, part, rim, tail, fine, rim_jacobian, points, out, faces_out, scratch):
    steps = field.shape[1]

    def step(b, u):
        lanes = lanes_of(b)
        total = rest_part(b, part, rim, tail, table, rim_jacobian)
        for a in range(NV):
            v = field[a, :, lanes] + points[pl.ds(a, 1), lanes] * total[a]
            for i in range(GROUP):
                scratch[u, a, pl.ds(i, steps, stride=GROUP), :] = v
            out[a, :, lanes] = fine[a, :, lanes] + scratch[u, a]

    each_block(table.shape[1], step)
    faces_kernel(listed, out, faces_out)


def residual_kernel(table, part, rim, tail, rim_jacobian, out, scratch, sems):
    blocks = table.shape[1]

    def send(b):
        lanes = lanes_of(b)
        return pltpu.make_async_copy(scratch.at[:, :, lanes], out.at[:, :, lanes], sems.at[b])

    def step(b, u):
        lanes = lanes_of(b)
        total = rest_part(b, part, rim, tail, table, rim_jacobian)
        for a in range(NV):
            scratch[a, :, lanes] = total[a]
        send(b).start()

    each_block(blocks, step)
    each_block(blocks, lambda b, u: send(b).wait())


def exchange(faces, tail):
    slabs, periods = lax.axis_size("space"), lax.axis_size("tm")
    across = [(i, i + 1) for i in range(1, slabs - 1, 2)]
    beside = [(i, i + 1) for i in range(0, slabs - 1, 2)]
    both_ways = lambda pairs: pairs + [(j, i) for i, j in pairs]
    rim_x = lax.ppermute(faces, "space", both_ways(across))
    rim_on = lax.ppermute(faces, "space", both_ways(beside))
    tail = lax.ppermute(tail, "tm", [(i, (i + 1) % periods) for i in range(periods)])
    return rim_x, rim_on, tail


def body(iterate, right_side, jacobian, self_block, cell_diag, neighbours, face_list):
    steps, cells = iterate.shape[0], iterate.shape[2]
    blocks, faces = cells // BLK, face_list.shape[0]
    coarse = steps // GROUP
    per_slot = 2 * blocks * NV * NV * BLK

    whole = lambda n: shape(NV, n, cells)
    face = lambda n: shape(faces, NV, n, BLK)
    rows_scratch = [pltpu.VMEM((UNROLL, NV, steps, BLK), jnp.float32)]

    table, listed = pl.pallas_call(
        table_kernel,
        out_shape=[pltpu.SMEM((K, blocks), jnp.int32), pltpu.SMEM((faces,), jnp.int32)],
        in_specs=[IN_SMEM] * 2,
        out_specs=[IN_SMEM] * 2,
        name="block_tables",
    )(jnp.transpose(neighbours), face_list)

    state = jnp.transpose(iterate, (1, 0, 2))
    goal = jnp.transpose(right_side, (1, 0, 2))
    jacobian = jnp.transpose(jacobian, (1, 2, 0, 3))
    fine_points, coarse_points = call(points_kernel, "point_diagonals", [], [cell_diag], [shape(NV, cells)] * 2)
    rim_jacobian = call(rim_jacobian_kernel, "rim_jacobian", [], [jacobian], [shape(2, NV, NV, cells)])[0]
    sent = call(faces_kernel, "faces_of_iterate", [listed], [state], [face(steps)])[0]

    def swap(sent, field, weight):
        tail = call(functools.partial(tail_kernel, weight), "tail", [], [field], [whole(2)])[0]
        return exchange(sent, tail)

    def own(weight, n, field, target, rim_on):
        return call(
            functools.partial(own_kernel, weight), "own_part", [table],
            [field, target, rim_on, jacobian, rim_jacobian, self_block, cell_diag], [whole(n)], 6 * per_slot * n,
        )[0]

    for sweep_no in range(NU1):
        rim_x, rim_on, tail = swap(sent, state, time_weight)
        part = own(time_weight, steps, state, goal, rim_on)
        arrays = [state, part, rim_x, tail, rim_jacobian, fine_points]
        if sweep_no < NU1 - 1:
            state, sent = call(
                sweep_kernel, "sweep", [table, listed], arrays, [whole(steps), face(steps)], per_slot * steps
            )
        else:
            state, means, sent = call(
                smoothed_kernel, "sweep_and_means", [table, listed], arrays,
                [whole(steps), whole(coarse), face(coarse)], per_slot * steps, rows_scratch,
            )

    rim_x, rim_on, tail = swap(sent, state, time_weight)
    part = call(
        functools.partial(means_kernel, time_weight), "own_part_of_means", [table],
        [state, goal, means, rim_on, jacobian, rim_jacobian, self_block, cell_diag], [whole(coarse)], 6 * per_slot * coarse,
        rows_scratch,
    )[0]
    defect, correction, sent = call(
        first_correction_kernel, "first_correction", [table, listed],
        [part, rim_x, tail, rim_jacobian, coarse_points], [whole(coarse), whole(coarse), face(coarse)], per_slot * coarse,
    )
    for sweep_no in range(NUC - 1):
        rim_x, rim_on, tail = swap(sent, correction, coarse_weight)
        part = own(coarse_weight, coarse, correction, defect, rim_on)
        if sweep_no < NUC - 2:
            correction, sent = call(
                sweep_kernel, "coarse_sweep", [table, listed],
                [correction, part, rim_x, tail, rim_jacobian, coarse_points],
                [whole(coarse), face(coarse)], per_slot * coarse,
            )
        else:
            state, sent = call(
                corrected_kernel, "corrected", [table, listed],
                [correction, part, rim_x, tail, state, rim_jacobian, coarse_points],
                [whole(steps), face(steps)], per_slot * coarse, rows_scratch,
            )

    for sweep_no in range(NU2):
        rim_x, rim_on, tail = swap(sent, state, time_weight)
        part = own(time_weight, steps, state, goal, rim_on)
        state, sent = call(
            sweep_kernel, "sweep", [table, listed],
            [state, part, rim_x, tail, rim_jacobian, fine_points], [whole(steps), face(steps)], per_slot * steps,
        )
    rim_x, rim_on, tail = swap(sent, state, time_weight)
    part = own(time_weight, steps, state, goal, rim_on)
    residual = call(
        residual_kernel, "residual", [table], [part, rim_x, tail, rim_jacobian], [whole(steps)], per_slot * steps,
        [pltpu.VMEM((NV, steps, cells), jnp.float32), pltpu.SemaphoreType.DMA((blocks,))],
        [pl.BlockSpec(memory_space=pl.ANY)],
    )[0]
    return jnp.transpose(state, (1, 0, 2)), jnp.transpose(residual, (1, 0, 2))


def solution(mesh):
    in_specs = (
        P("tm", None, "space"),
        P("tm", None, "space"),
        P(None, None, None, "space"),
        P(None, None, "space"),
        P(None, "space"),
        P("space", None),
        P("space"),
    )
    out_specs = (P("tm", None, "space"), P("tm", None, "space"))
    return jax.shard_map(body, mesh=mesh, in_specs=in_specs, out_specs=out_specs, check_vma=False)
```

```python
import functools

import jax
import jax.numpy as jnp
from jax import lax
from jax.experimental import pallas as pl
from jax.experimental.pallas import tpu as pltpu
from jax.sharding import PartitionSpec as P

NV = 5
BLK = 128
K = 6
NU1 = 2
NU2 = 2
NUC = 4
GROUP = 4

time_weight = 0.5
coarse_weight = time_weight / GROUP
damping = 0.7

UNROLL = 4
SCRATCH_BYTES = 4 << 20
IN_VMEM = pl.BlockSpec(memory_space=pltpu.VMEM)
NOTHING = pl.CostEstimate(flops=1, bytes_accessed=1, transcendentals=0)
LONG = pl.CostEstimate(flops=0, bytes_accessed=100 << 20, transcendentals=0)
IN_HBM = pl.BlockSpec(memory_space=pltpu.HBM)
IN_SMEM = pl.BlockSpec(memory_space=pltpu.SMEM)


def call(kernel, name, tables, arrays, outs, flops=0, scratch=(), out_specs=None):
    arrays = [pltpu.with_memory_space_constraint(a, pltpu.VMEM) for a in arrays]
    size = 4 * (sum(a.size for a in arrays) + sum(o.size for o in outs))
    return pl.pallas_call(
        kernel,
        out_shape=outs if out_specs else [pltpu.VMEM(o.shape, o.dtype) for o in outs],
        in_specs=[IN_SMEM] * len(tables) + [IN_VMEM] * len(arrays),
        out_specs=out_specs or [IN_VMEM] * len(outs),
        scratch_shapes=scratch,
        cost_estimate=LONG if name.startswith('rim') else NOTHING,
        compiler_params=pltpu.CompilerParams(vmem_limit_bytes=SCRATCH_BYTES),
        name=name,
    )(*tables, *arrays)


def in_hbm(array):
    return pltpu.with_memory_space_constraint(array, pltpu.HBM)


def shape(*dims):
    return jax.ShapeDtypeStruct(dims, jnp.float32)


def lanes_of(b):
    return pl.ds(pl.multiple_of(b * BLK, BLK), BLK)


def cross_slot():
    return lax.rem(lax.axis_index("space"), 2)


def each_block(count, step):
    unroll = UNROLL if count % UNROLL == 0 else 1

    def steps(i, carry):
        for u in range(unroll):
            step(i * unroll + u, u)
        return carry

    lax.fori_loop(0, count // unroll, steps, 0)


def first_kernel(neighbours, face_list, iterate, table, listed, field, faces_out, near, named, sems):
    copies = [
        pltpu.make_async_copy(iterate, field, sems.at[0]),
        pltpu.make_async_copy(neighbours, near, sems.at[1]),
        pltpu.make_async_copy(face_list, named, sems.at[2]),
    ]
    for copy in copies:
        copy.start()
    slot = cross_slot()
    slots, blocks = near.shape
    faces = named.shape[0]
    copies[1].wait()

    def step(b, carry):
        table[0, b] = near[slot, b] - (blocks + faces * slot)
        table[1, b] = near[1 - slot, b] - (blocks + faces * (1 - slot))
        for k in range(2, slots):
            table[k, b] = near[k, b]
        return carry

    lax.fori_loop(0, blocks, step, 0)
    copies[2].wait()
    for h in range(faces):
        listed[h] = named[h]
    copies[0].wait()
    pick_faces(listed, field, faces_out)


def arguments_kernel(listed, *refs):
    arguments, held = refs[:4], refs[4:8]
    fine_out, coarse_out, out, sems = refs[8:]
    copies = [pltpu.make_async_copy(x, y, sems.at[i]) for i, (x, y) in enumerate(zip(arguments, held))]
    for copy in copies:
        copy.start()
    for copy in copies:
        copy.wait()
    cell_diag, jacobian = held[0], held[1]
    fine_out[...] = damping / (3.0 * time_weight + cell_diag[...])
    coarse_out[...] = damping / (3.0 * coarse_weight + cell_diag[...])
    lower_crosses = cross_slot() == 0
    for a in range(NV):
        for j in range(NV):
            lower, upper = jacobian[a, j, pl.ds(0, 1), :], jacobian[a, j, pl.ds(1, 1), :]
            out[0, a, pl.ds(j, 1), :] = jnp.where(lower_crosses, lower, upper)
            out[1, a, pl.ds(j, 1), :] = jnp.where(lower_crosses, upper, lower)


def coupled(total, coupling, values):
    for j in range(NV):
        for a in range(NV):
            total[a] = total[a] - coupling(a, j) * values[j]
    return total


def earlier(v, steps):
    if v.shape[0] <= steps:
        return jnp.zeros_like(v)
    return jnp.concatenate([jnp.zeros((steps, BLK), jnp.float32), v[: v.shape[0] - steps]], axis=0)


def own_part(total, b, field, table, jacobian, self_block):
    lanes = lanes_of(b)
    v = [field[j, :, lanes] for j in range(NV)]
    for a in range(NV):
        for j in range(NV):
            if j != a:
                total[a] = total[a] - self_block[a, pl.ds(j, 1), lanes] * v[j]
    for slot in range(2, K):
        there = lanes_of(table[slot, b])
        row = pl.ds(slot, 1)
        total = coupled(total, lambda a, j: jacobian[a, j, row, lanes], [field[j, :, there] for j in range(NV)])
    return total


def rim_part(side, total, b, rim, table, rim_jacobian):
    block, lanes = table[side, b], lanes_of(b)
    coupling = lambda a, j: rim_jacobian[side, a, pl.ds(j, 1), lanes]
    return coupled(total, coupling, [rim[block, j] for j in range(NV)])


def pick_faces(listed, field, faces_out):
    for h in range(listed.shape[0]):
        lanes = lanes_of(listed[h])
        for a in range(NV):
            faces_out[h, a] = field[a, :, lanes]


def tail_rows(last_two, weight):
    last = last_two[1:]
    return weight * jnp.concatenate([last_two[:1] - 4.0 * last, last], axis=0)


def tail_kernel(weight, rim_weight, field, *refs):
    steps, cells = field.shape[1:]
    tail_out = refs[-1]
    for a in range(NV):
        last = field[a, pl.ds(steps - 1, 1), :]
        tail_out[a, pl.ds(0, 1), pl.ds(0, cells)] = weight * (field[a, pl.ds(steps - 2, 1), :] - 4.0 * last)
        tail_out[a, pl.ds(1, 1), pl.ds(0, cells)] = weight * last
    if len(refs) > 1:
        rim = refs[0]
        for h in range(rim.shape[0]):
            for a in range(NV):
                rows = tail_rows(rim[h, a, pl.ds(rim.shape[2] - 2, 2), :], rim_weight)
                tail_out[a, :, pl.ds(cells + h * BLK, BLK)] = rows


def own_kernel(weight, table, field, goal, jacobian, self_block, cell_diag, out):
    def step(b, u):
        lanes = lanes_of(b)
        total = []
        for a in range(NV):
            v = field[a, :, lanes]
            point = 3.0 * weight + cell_diag[pl.ds(a, 1), lanes]
            timed = weight * (earlier(v, 2) - 4.0 * earlier(v, 1))
            total.append(goal[a, :, lanes] - point * v - timed)
        total = own_part(total, b, field, table, jacobian, self_block)
        for a in range(NV):
            out[a, :, lanes] = total[a]

    each_block(table.shape[1], step)


def mean_rows(v, scratch, steps):
    scratch[...] = v
    return sum(scratch[pl.ds(i, steps, stride=GROUP), :] for i in range(GROUP)) * (1.0 / GROUP)


def spread_rows(v, scratch):
    for i in range(GROUP):
        scratch[pl.ds(i, v.shape[0], stride=GROUP), :] = v
    return scratch[...]


def means_kernel(weight, table, field, goal, means, jacobian, self_block, cell_diag, out, scratch):
    steps = means.shape[1]

    def step(b, u):
        lanes = lanes_of(b)
        total = []
        for a in range(NV):
            v = field[a, :, lanes]
            fine = goal[a, :, lanes] - weight * (3.0 * v - 4.0 * earlier(v, 1) + earlier(v, 2))
            total.append(mean_rows(fine, scratch.at[u, a], steps) - cell_diag[pl.ds(a, 1), lanes] * means[a, :, lanes])
        total = own_part(total, b, means, table, jacobian, self_block)
        for a in range(NV):
            out[a, :, lanes] = total[a]

    each_block(table.shape[1], step)


def beside_part(table, part, rim, rim_jacobian, out):
    def step(b, u):
        lanes = lanes_of(b)
        total = rim_part(1, [part[a, :, lanes] for a in range(NV)], b, rim, table, rim_jacobian)
        for a in range(NV):
            out[a, :, lanes] = total[a]

    each_block(table.shape[1], step)


def step_of(listed, h, a, field, part, points):
    lanes = lanes_of(listed[h])
    return field[a, :, lanes] + points[pl.ds(a, 1), lanes] * part[a, :, lanes]


def message_kernel(table, listed, field, part, rim, rim_jacobian, points, out, message):
    beside_part(table, part, rim, rim_jacobian, out)
    for h in range(listed.shape[0]):
        for a in range(NV):
            message[h, a] = step_of(listed, h, a, field, out, points)


def first_message_kernel(
    table, listed, field, part, rim, rim_jacobian, points, coarse_points, tail, out, message
):
    beside_part(table, part, rim, rim_jacobian, out)
    steps = field.shape[1]
    behind = NV * steps
    for h in range(listed.shape[0]):
        block = listed[h]
        lanes = lanes_of(block)
        for a in range(NV):
            message[h, pl.ds(a * steps, steps), :] = step_of(listed, h, a, field, out, points)
            message[h, pl.ds(behind + NV * a, NV), :] = rim_jacobian[0, a, :, lanes]
        message[h, pl.ds(behind + NV * NV, NV), :] = points[:, lanes]
        message[h, pl.ds(behind + NV * NV + NV, NV), :] = coarse_points[:, lanes]
        named = jnp.full((1, BLK), table[0, block], jnp.int32)
        message[h, pl.ds(behind + NV * NV + 2 * NV, 1), :] = named.astype(jnp.float32)


def means_message_kernel(table, listed, field, part, rim, rim_jacobian, points, out, message, scratch):
    beside_part(table, part, rim, rim_jacobian, out)
    steps = field.shape[1]
    coarse = steps // GROUP
    for h in range(listed.shape[0]):
        for a in range(NV):
            v = step_of(listed, h, a, field, out, points)
            message[h, a, pl.ds(0, coarse), :] = mean_rows(v, scratch.at[h % UNROLL, a], coarse)
            message[h, a, pl.ds(coarse, 2), :] = v[steps - 2 :]


def scaled_message_kernel(table, listed, part, rim, rim_jacobian, points, out, message):
    beside_part(table, part, rim, rim_jacobian, out)
    for h in range(listed.shape[0]):
        lanes = lanes_of(listed[h])
        for a in range(NV):
            message[h, a] = points[pl.ds(a, 1), lanes] * out[a, :, lanes]


def corrected_message_kernel(table, listed, field, part, rim, fine, rim_jacobian, points, out, message, scratch):
    beside_part(table, part, rim, rim_jacobian, out)
    for h in range(listed.shape[0]):
        for a in range(NV):
            v = step_of(listed, h, a, field, out, points)
            message[h, a] = fine[a, :, lanes_of(listed[h])] + spread_rows(v, scratch.at[h % UNROLL, a])


class Partner:
    def __init__(self, ref, steps, level):
        self.ref, self.behind, self.level = ref, NV * steps, level

    def row(self, h, r):
        return self.ref[h, pl.ds(self.behind + r, 1), :]

    def coupling(self, h):
        return lambda a, j: self.row(h, NV * a + j)

    def point(self, h, a):
        return self.row(h, NV * (NV + self.level) + a)


def index_kernel(steps, message, index):
    partner = Partner(message, steps, 0)
    for h in range(index.shape[0]):
        index[h] = jnp.max(partner.row(h, NV * (NV + 2))).astype(jnp.int32)


def own_share(index, h, faces, partner):
    block = index[h]
    zero = [jnp.zeros(faces.shape[2:], jnp.float32)] * NV
    total = coupled(zero, partner.coupling(h), [faces[block, j] for j in range(NV)])
    return [partner.point(h, a) * total[a] for a in range(NV)]


def rim_kernel(steps, level, index, faces, message, first_message, out):
    partner = Partner(first_message, steps, level)

    def step(h, u):
        share = own_share(index, h, faces, partner)
        for a in range(NV):
            if len(message.shape) == 3:
                out[h, a] = message[h, pl.ds(a * steps, steps), :] + share[a]
            else:
                out[h, a] = message[h, a] + share[a]

    each_block(index.shape[0], step)


def means_rim_kernel(steps, index, faces, message, first_message, out, last_out, scratch):
    partner = Partner(first_message, steps, 0)
    coarse = out.shape[2]

    def step(h, u):
        share = own_share(index, h, faces, partner)
        for a in range(NV):
            out[h, a] = message[h, a, pl.ds(0, coarse), :] + mean_rows(share[a], scratch.at[u, a], coarse)
            last_out[h, a] = message[h, a, pl.ds(coarse, 2), :] + share[a][steps - 2 :]

    each_block(index.shape[0], step)


def corrected_rim_kernel(steps, index, faces, message, first_message, out, scratch):
    partner = Partner(first_message, steps, 1)

    def step(h, u):
        share = own_share(index, h, faces, partner)
        for a in range(NV):
            out[h, a] = message[h, a] + spread_rows(share[a], scratch.at[u, a])

    each_block(index.shape[0], step)


def less_rows(total, rows):
    pad = total.shape[0] - rows.shape[0]
    if pad:
        rows = jnp.concatenate([rows, jnp.zeros((pad, BLK), jnp.float32)], axis=0)
    return total - rows


def mean_tail(rows):
    return (rows[:1] + rows[1:]) * (1.0 / GROUP)


def spread_tail(rows):
    return jnp.concatenate([jnp.broadcast_to(rows[i : i + 1], (GROUP, BLK)) for i in range(2)], axis=0)


def finish_rim(rim, tail, cells, partner, shape_tail, rim_out):
    def step(h, u):
        lanes = pl.ds(pl.multiple_of(cells + h * BLK, BLK), BLK)
        for a in range(NV):
            rim_out[h, a] = less_rows(rim[h, a], shape_tail(partner.point(h, a) * tail[a, :, lanes]))

    each_block(rim.shape[0], step)


def rest_part(b, part, rim, tail, table, rim_jacobian, shape_tail=lambda rows: rows):
    lanes = lanes_of(b)
    total = [less_rows(part[a, :, lanes], shape_tail(tail[a, :, lanes])) for a in range(NV)]
    return rim_part(0, total, b, rim, table, rim_jacobian)


def first_sweep_kernel(table, listed, field, part, rim, tail, rim_jacobian, points, out, faces_out):
    def step(b, u):
        lanes = lanes_of(b)
        total = rest_part(b, part, rim, tail, table, rim_jacobian)
        for a in range(NV):
            out[a, :, lanes] = field[a, :, lanes] + points[pl.ds(a, 1), lanes] * total[a]

    each_block(table.shape[1], step)
    pick_faces(listed, out, faces_out)


def sweep_kernel(
    steps, level, shape_tail, table, listed, field, part, rim, tail, first_message, rim_jacobian, points,
    out, faces_out, rim_out,
):
    finish_rim(rim, tail, field.shape[2], Partner(first_message, steps, level), shape_tail, rim_out)
    first_sweep_kernel(table, listed, field, part, rim_out, tail, rim_jacobian, points, out, faces_out)


def smoothed_kernel(
    table, listed, field, part, rim, tail, first_message, rim_jacobian, points,
    out, means_out, faces_out, rim_out, scratch,
):
    steps = means_out.shape[1]
    partner = Partner(first_message, field.shape[1], 0)
    finish_rim(rim, tail, field.shape[2], partner, lambda rows: rows, rim_out)

    def step(b, u):
        lanes = lanes_of(b)
        total = rest_part(b, part, rim_out, tail, table, rim_jacobian)
        for a in range(NV):
            v = field[a, :, lanes] + points[pl.ds(a, 1), lanes] * total[a]
            out[a, :, lanes] = v
            means_out[a, :, lanes] = mean_rows(v, scratch.at[u, a], steps)

    each_block(table.shape[1], step)
    pick_faces(listed, means_out, faces_out)


def first_correction_kernel(
    steps, table, listed, part, rim, tail, first_message, rim_jacobian, points, defect_out, out, faces_out, rim_out
):
    finish_rim(rim, tail, part.shape[2], Partner(first_message, steps, 0), mean_tail, rim_out)

    def step(b, u):
        lanes = lanes_of(b)
        total = rest_part(b, part, rim_out, tail, table, rim_jacobian, mean_tail)
        for a in range(NV):
            defect_out[a, :, lanes] = total[a]
            out[a, :, lanes] = points[pl.ds(a, 1), lanes] * total[a]

    each_block(table.shape[1], step)
    pick_faces(listed, out, faces_out)


def corrected_kernel(
    steps, table, listed, field, part, rim, tail, fine, first_message, rim_jacobian, points,
    out, faces_out, rim_out, scratch,
):
    partner = Partner(first_message, steps, 1)
    finish_rim(rim, tail, field.shape[2], partner, lambda rows: rows, rim_out)

    def step(b, u):
        lanes = lanes_of(b)
        total = rest_part(b, part, rim_out, tail, table, rim_jacobian)
        for a in range(NV):
            v = field[a, :, lanes] + points[pl.ds(a, 1), lanes] * total[a]
            out[a, :, lanes] = fine[a, :, lanes] + spread_rows(v, scratch.at[u, a])

    each_block(table.shape[1], step)
    pick_faces(listed, out, faces_out)


def residual_kernel(
    steps, table, field, part, rim, tail, first_message, rim_jacobian, updated, out, scratch, finished, sems
):
    blocks = table.shape[1]
    copy = pltpu.make_async_copy(field, updated, sems.at[blocks])
    copy.start()
    partner = Partner(first_message, steps, 0)
    finish_rim(rim, tail, part.shape[2], partner, lambda rows: rows, finished)

    def send(b):
        lanes = lanes_of(b)
        return pltpu.make_async_copy(scratch.at[:, :, lanes], out.at[:, :, lanes], sems.at[b])

    def step(b, u):
        lanes = lanes_of(b)
        total = rest_part(b, part, finished, tail, table, rim_jacobian)
        for a in range(NV):
            scratch[a, :, lanes] = total[a]
        send(b).start()

    each_block(blocks, step)
    each_block(blocks, lambda b, u: send(b).wait())
    copy.wait()


def neighbour_pairs(first):
    pairs = [(i, i + 1) for i in range(first, lax.axis_size("space") - 1, 2)]
    return pairs + [(j, i) for i, j in pairs]


def over_chips(message):
    return lax.ppermute(message, "space", neighbour_pairs(1))


def on_chip(faces):
    return lax.ppermute(faces, "space", neighbour_pairs(0))


def to_later(tail):
    periods = lax.axis_size("tm")
    return lax.ppermute(tail, "tm", [(i, (i + 1) % periods) for i in range(periods)])


def body(iterate, right_side, jacobian, self_block, cell_diag, neighbours, face_list):
    steps, cells = iterate.shape[0], iterate.shape[2]
    blocks, faces = cells // BLK, face_list.shape[0]
    coarse = steps // GROUP
    per_slot = 2 * blocks * NV * NV * BLK

    whole = lambda n: shape(NV, n, cells)
    face = lambda n: shape(faces, NV, n, BLK)
    spare = lambda more, n: shape(faces + more, NV, n, BLK)
    rows_scratch = [pltpu.VMEM((UNROLL, NV, steps, BLK), jnp.float32)]
    bind = functools.partial
    plain = lambda rows: rows

    goal = jnp.transpose(right_side, (1, 0, 2))
    jacobian = jnp.transpose(jacobian, (1, 2, 0, 3))
    table, listed, start, sent = pl.pallas_call(
        first_kernel,
        out_shape=[
            pltpu.SMEM((K, blocks), jnp.int32), pltpu.SMEM((faces,), jnp.int32),
            pltpu.VMEM((NV, steps, cells), jnp.float32), pltpu.VMEM((faces, NV, steps, BLK), jnp.float32),
        ],
        in_specs=[IN_HBM] * 3,
        out_specs=[IN_SMEM] * 2 + [IN_VMEM] * 2,
        scratch_shapes=[
            pltpu.SMEM((K, blocks), jnp.int32), pltpu.SMEM((faces,), jnp.int32), pltpu.SemaphoreType.DMA((3,)),
        ],
        compiler_params=pltpu.CompilerParams(vmem_limit_bytes=SCRATCH_BYTES),
        cost_estimate=NOTHING,
        name="iterate_and_tables",
    )(*[in_hbm(x) for x in (jnp.transpose(neighbours), face_list, jnp.transpose(iterate, (1, 0, 2)))])
    tables = [table, listed]
    rim = over_chips(sent)
    beside = on_chip(sent)
    arguments = [in_hbm(x) for x in (cell_diag, jacobian, self_block, goal)]
    outs = [shape(*x.shape) for x in arguments] + [shape(NV, cells)] * 2 + [shape(2, NV, NV, cells)]
    cell_diag, jacobian, self_block, goal, fine_points, coarse_points, rim_jacobian = pl.pallas_call(
        arguments_kernel,
        out_shape=[pltpu.VMEM(x.shape, jnp.float32) for x in outs],
        in_specs=[IN_SMEM] + [IN_HBM] * len(arguments),
        out_specs=[IN_VMEM] * len(outs),
        scratch_shapes=[pltpu.SemaphoreType.DMA((len(arguments),))],
        compiler_params=pltpu.CompilerParams(vmem_limit_bytes=SCRATCH_BYTES),
        cost_estimate=NOTHING,
        name="arguments",
    )(listed, *arguments)

    def own(weight, n, field, target):
        return call(
            bind(own_kernel, weight), "own_part", [table], [field, target, jacobian, self_block, cell_diag],
            [whole(n)], 5 * per_slot * n,
        )[0]

    def tail_of(field, weight, rim=None, rim_weight=None):
        arrays = [field] if rim is None else [field, rim]
        out = shape(NV, 2, cells + (0 if rim is None else faces * BLK))
        return to_later(call(bind(tail_kernel, weight, rim_weight), "tail", [], arrays, [out])[0])

    state = start
    tail = tail_of(state, time_weight)
    part = own(time_weight, steps, state, goal)
    part, message = call(
        first_message_kernel, "first_message", tables,
        [state, part, beside, rim_jacobian, fine_points, coarse_points, tail],
        [whole(steps), shape(faces, NV * steps + NV * (NV + 3), BLK)], per_slot * steps,
    )
    first_message = over_chips(message)
    message = first_message
    earlier_sent = sent
    state, sent = call(
        first_sweep_kernel, "first_sweep", tables, [state, part, rim, tail, rim_jacobian, fine_points],
        [whole(steps), face(steps)], per_slot * steps,
    )
    index = pl.pallas_call(
        bind(index_kernel, steps), out_shape=pltpu.SMEM((faces,), jnp.int32), in_specs=[IN_VMEM],
        out_specs=IN_SMEM, name="coupled_faces", cost_estimate=NOTHING,
        compiler_params=pltpu.CompilerParams(vmem_limit_bytes=SCRATCH_BYTES),
    )(pltpu.with_memory_space_constraint(first_message, pltpu.VMEM))

    beside = on_chip(sent)
    tail = tail_of(state, time_weight, rim, time_weight)
    part = own(time_weight, steps, state, goal)
    part, next_message = call(
        means_message_kernel, "message_of_means", tables, [state, part, beside, rim_jacobian, fine_points],
        [whole(steps), face(coarse + 2)], per_slot * steps, rows_scratch,
    )
    next_message = over_chips(next_message)
    rim = call(
        bind(rim_kernel, steps, 0), "rim", [index], [earlier_sent, message, first_message], [face(steps)],
        per_slot * steps // 2,
    )[0]
    message, earlier_sent = next_message, sent
    state, means, sent, rim = call(
        smoothed_kernel, "sweep_and_means", tables,
        [state, part, rim, tail, first_message, rim_jacobian, fine_points],
        [whole(steps), whole(coarse), face(coarse), face(steps)], per_slot * steps, rows_scratch,
    )

    beside = on_chip(sent)
    tail = tail_of(state, time_weight, rim, time_weight)
    part = call(
        bind(means_kernel, time_weight), "own_part_of_means", [table],
        [state, goal, means, jacobian, self_block, cell_diag], [whole(coarse)], 5 * per_slot * coarse, rows_scratch,
    )[0]
    part, next_message = call(
        scaled_message_kernel, "message_of_correction", tables, [part, beside, rim_jacobian, coarse_points],
        [whole(coarse), spare(faces, coarse)], per_slot * coarse,
    )
    next_message = over_chips(next_message)
    rim, last_rows = call(
        bind(means_rim_kernel, steps), "rim_of_means", [index], [earlier_sent, message, first_message],
        [face(coarse), face(2)], per_slot * steps // 2, rows_scratch,
    )
    message, earlier_sent = next_message, sent
    defect, correction, sent, rim = call(
        bind(first_correction_kernel, steps), "first_correction", tables,
        [part, rim, tail, first_message, rim_jacobian, coarse_points],
        [whole(coarse), whole(coarse), face(coarse), face(coarse)], per_slot * coarse,
    )

    rim, rim_weight, shape_tail = last_rows, time_weight, mean_tail
    for sweep_no in range(NUC - 1):
        beside = on_chip(sent)
        tail = tail_of(correction, coarse_weight, rim, rim_weight)
        part = own(coarse_weight, coarse, correction, defect)
        last = sweep_no == NUC - 2
        if last:
            part, next_message = call(
                corrected_message_kernel, "message_of_corrected", tables,
                [correction, part, beside, state, rim_jacobian, coarse_points],
                [whole(coarse), spare(1, steps)], per_slot * coarse, rows_scratch,
            )
        else:
            part, next_message = call(
                message_kernel, "message_of_coarse", tables, [correction, part, beside, rim_jacobian, coarse_points],
                [whole(coarse), spare(faces, coarse)], per_slot * coarse,
            )
        next_message = over_chips(next_message)
        rim = call(
            bind(rim_kernel, steps, 1), "rim_of_coarse", [index], [earlier_sent, message, first_message],
            [face(coarse)], per_slot * coarse // 2,
        )[0]
        message, earlier_sent = next_message, sent
        if last:
            state, sent, rim = call(
                bind(corrected_kernel, steps), "corrected", tables,
                [correction, part, rim, tail, state, first_message, rim_jacobian, coarse_points],
                [whole(steps), face(steps), face(coarse)], per_slot * coarse, rows_scratch,
            )
        else:
            correction, sent, rim = call(
                bind(sweep_kernel, steps, 1, shape_tail), "coarse_sweep", tables,
                [correction, part, rim, tail, first_message, rim_jacobian, coarse_points],
                [whole(coarse), face(coarse), face(coarse)], per_slot * coarse,
            )
        rim_weight, shape_tail = coarse_weight, plain

    for sweep_no in range(NU2 + 1):
        beside = on_chip(sent)
        tail = tail_of(state, time_weight, rim, rim_weight)
        part = own(time_weight, steps, state, goal)
        last = sweep_no == NU2
        if last:
            part = call(
                beside_part, "beside_part", [table], [part, beside, rim_jacobian], [whole(steps)], per_slot * steps
            )[0]
        else:
            part, next_message = call(
                message_kernel, "message", tables, [state, part, beside, rim_jacobian, fine_points],
                [whole(steps), spare(1, steps)], per_slot * steps,
            )
            next_message = over_chips(next_message)
        if sweep_no == 0:
            rim = call(
                bind(corrected_rim_kernel, steps), "rim_of_corrected", [index],
                [earlier_sent, message, first_message], [face(steps)], per_slot * coarse // 2, rows_scratch,
            )[0]
            level, shape_tail = 1, spread_tail
        else:
            rim = call(
                bind(rim_kernel, steps, 0), "rim", [index], [earlier_sent, message, first_message],
                [face(steps)], per_slot * steps // 2,
            )[0]
            level, shape_tail = 0, plain
        if not last:
            message, earlier_sent = next_message, sent
            state, sent, rim = call(
                bind(sweep_kernel, steps, level, shape_tail), "sweep", tables,
                [state, part, rim, tail, first_message, rim_jacobian, fine_points],
                [whole(steps), face(steps), face(steps)], per_slot * steps,
            )
        rim_weight = time_weight
    updated, residual = call(
        bind(residual_kernel, steps), "residual", [table], [state, part, rim, tail, first_message, rim_jacobian],
        [whole(steps)] * 2, per_slot * steps,
        [
            pltpu.VMEM((NV, steps, cells), jnp.float32), pltpu.VMEM((faces, NV, steps, BLK), jnp.float32),
            pltpu.SemaphoreType.DMA((blocks + 1,)),
        ],
        [IN_HBM] * 2,
    )
    return jnp.transpose(updated, (1, 0, 2)), jnp.transpose(residual, (1, 0, 2))


def solution(mesh):
    in_specs = (
        P("tm", None, "space"),
        P("tm", None, "space"),
        P(None, None, None, "space"),
        P(None, None, "space"),
        P(None, "space"),
        P("space", None),
        P("space"),
    )
    out_specs = (P("tm", None, "space"), P("tm", None, "space"))
    return jax.shard_map(body, mesh=mesh, in_specs=in_specs, out_specs=out_specs, check_vma=False)
```

```python
import functools

import jax
import jax.numpy as jnp
from jax import lax
from jax.experimental import pallas as pl
from jax.experimental.pallas import tpu as pltpu
from jax.sharding import PartitionSpec as P

NV = 5
BLK = 128
K = 6
NU1 = 2
NU2 = 2
NUC = 4
GROUP = 4

time_weight = 0.5
coarse_weight = time_weight / GROUP
damping = 0.7

UNROLL = 8
SCRATCH_BYTES = 4 << 20
IN_VMEM = pl.BlockSpec(memory_space=pltpu.VMEM)
NOTHING = pl.CostEstimate(flops=1, bytes_accessed=1, transcendentals=0)
LONG = pl.CostEstimate(flops=0, bytes_accessed=100 << 20, transcendentals=0)
IN_HBM = pl.BlockSpec(memory_space=pltpu.HBM)
IN_SMEM = pl.BlockSpec(memory_space=pltpu.SMEM)


def call(kernel, name, tables, arrays, outs, flops=0, scratch=(), out_specs=None, in_place=0):
    arrays = [pltpu.with_memory_space_constraint(a, pltpu.VMEM) for a in arrays]
    size = 4 * (sum(a.size for a in arrays) + sum(o.size for o in outs))
    return pl.pallas_call(
        kernel,
        out_shape=[
            o if out_specs and out_specs[i] is IN_HBM else pltpu.VMEM(o.shape, o.dtype) for i, o in enumerate(outs)
        ],
        in_specs=[IN_SMEM] * len(tables) + [IN_VMEM] * len(arrays),
        out_specs=out_specs or [IN_VMEM] * len(outs),
        scratch_shapes=scratch,
        input_output_aliases={len(tables) + i: i for i in range(in_place)},
        cost_estimate=LONG if name.startswith('rim') else NOTHING,
        compiler_params=pltpu.CompilerParams(vmem_limit_bytes=SCRATCH_BYTES),
        name=name,
    )(*tables, *arrays)


def in_hbm(array):
    return pltpu.with_memory_space_constraint(array, pltpu.HBM)


def shape(*dims):
    return jax.ShapeDtypeStruct(dims, jnp.float32)


def lanes_of(b):
    return pl.ds(pl.multiple_of(b * BLK, BLK), BLK)


def cross_slot():
    return lax.rem(lax.axis_index("space"), 2)


def each_block(count, step):
    unroll = UNROLL if count % UNROLL == 0 else 1

    def steps(i, carry):
        for u in range(unroll):
            step(i * unroll + u, u)
        return carry

    lax.fori_loop(0, count // unroll, steps, 0)


def first_kernel(neighbours, face_list, iterate, table, listed, field, faces_out, near, named, sems):
    copies = [
        pltpu.make_async_copy(iterate, field, sems.at[0]),
        pltpu.make_async_copy(neighbours, near, sems.at[1]),
        pltpu.make_async_copy(face_list, named, sems.at[2]),
    ]
    for copy in copies:
        copy.start()
    slot = cross_slot()
    slots, blocks = near.shape
    faces = named.shape[0]
    copies[1].wait()

    def step(b, carry):
        table[0, b] = near[slot, b] - (blocks + faces * slot)
        table[1, b] = near[1 - slot, b] - (blocks + faces * (1 - slot))
        for k in range(2, slots):
            table[k, b] = near[k, b]
        return carry

    lax.fori_loop(0, blocks, step, 0)
    copies[2].wait()
    for h in range(faces):
        listed[h] = named[h]
    copies[0].wait()
    pick_faces(listed, field, faces_out)


def arguments_kernel(listed, *refs):
    arguments, held = refs[:4], refs[4:8]
    fine_out, coarse_out, out, sems = refs[8:]
    copies = [pltpu.make_async_copy(x, y, sems.at[i]) for i, (x, y) in enumerate(zip(arguments, held))]
    for copy in copies:
        copy.start()
    for copy in copies:
        copy.wait()
    cell_diag, jacobian = held[0], held[1]
    fine_out[...] = damping / (3.0 * time_weight + cell_diag[...])
    coarse_out[...] = damping / (3.0 * coarse_weight + cell_diag[...])
    lower_crosses = cross_slot() == 0
    for a in range(NV):
        for j in range(NV):
            lower, upper = jacobian[a, j, pl.ds(0, 1), :], jacobian[a, j, pl.ds(1, 1), :]
            out[0, a, pl.ds(j, 1), :] = jnp.where(lower_crosses, lower, upper)
            out[1, a, pl.ds(j, 1), :] = jnp.where(lower_crosses, upper, lower)


def coupled(total, coupling, values):
    for j in range(NV):
        for a in range(NV):
            total[a] = total[a] - coupling(a, j) * values[j]
    return total


def earlier(v, steps):
    if v.shape[0] <= steps:
        return jnp.zeros_like(v)
    return jnp.concatenate([jnp.zeros((steps, BLK), jnp.float32), v[: v.shape[0] - steps]], axis=0)


def own_part(total, b, field, table, jacobian, self_block):
    lanes = lanes_of(b)
    v = [field[j, :, lanes] for j in range(NV)]
    for a in range(NV):
        for j in range(NV):
            if j != a:
                total[a] = total[a] - self_block[a, pl.ds(j, 1), lanes] * v[j]
    for slot in range(2, K):
        there = lanes_of(table[slot, b])
        row = pl.ds(slot, 1)
        total = coupled(total, lambda a, j: jacobian[a, j, row, lanes], [field[j, :, there] for j in range(NV)])
    return total


def rim_part(side, total, b, rim, table, rim_jacobian):
    block, lanes = table[side, b], lanes_of(b)
    coupling = lambda a, j: rim_jacobian[side, a, pl.ds(j, 1), lanes]
    return coupled(total, coupling, [rim[block, j] for j in range(NV)])


def pick_faces(listed, field, faces_out):
    for h in range(listed.shape[0]):
        lanes = lanes_of(listed[h])
        for a in range(NV):
            faces_out[h, a] = field[a, :, lanes]


def tail_rows(last_two, weight, mean):
    last = last_two[1:]
    if mean:
        return jnp.concatenate([(weight / GROUP) * (last_two[:1] - 3.0 * last), jnp.zeros_like(last)], axis=0)
    return weight * jnp.concatenate([last_two[:1] - 4.0 * last, last], axis=0)


def send_tail(weights, field, rim, tail_out):
    steps, cells = field.shape[1:]
    weight, mean, rim_weight, rim_mean = weights
    for a in range(NV):
        before, last = field[a, pl.ds(steps - 2, 1), :], field[a, pl.ds(steps - 1, 1), :]
        if mean:
            tail_out[a, pl.ds(0, 1), pl.ds(0, cells)] = (weight / GROUP) * (before - 3.0 * last)
            tail_out[a, pl.ds(1, 1), pl.ds(0, cells)] = jnp.zeros_like(last)
        else:
            tail_out[a, pl.ds(0, 1), pl.ds(0, cells)] = weight * (before - 4.0 * last)
            tail_out[a, pl.ds(1, 1), pl.ds(0, cells)] = weight * last
    if rim is not None:
        for h in range((tail_out.shape[2] - cells) // BLK):
            for a in range(NV):
                rows = tail_rows(rim[h, a, pl.ds(rim.shape[2] - 2, 2), :], rim_weight, rim_mean)
                tail_out[a, :, pl.ds(cells + h * BLK, BLK)] = rows


def tail_kernel(weights, field, *refs):
    send_tail(weights, field, refs[0] if len(refs) > 1 else None, refs[-1])


def own_kernel(weight, table, field, goal, jacobian, self_block, cell_diag, out):
    def step(b, u):
        lanes = lanes_of(b)
        total = []
        for a in range(NV):
            v = field[a, :, lanes]
            point = 3.0 * weight + cell_diag[pl.ds(a, 1), lanes]
            timed = weight * (earlier(v, 2) - 4.0 * earlier(v, 1))
            total.append(goal[a, :, lanes] - point * v - timed)
        total = own_part(total, b, field, table, jacobian, self_block)
        for a in range(NV):
            out[a, :, lanes] = total[a]

    each_block(table.shape[1], step)


def mean_rows(v, scratch, steps):
    scratch[...] = v
    return sum(scratch[pl.ds(i, steps, stride=GROUP), :] for i in range(GROUP)) * (1.0 / GROUP)


def spread_rows(v, scratch):
    for i in range(GROUP):
        scratch[pl.ds(i, v.shape[0], stride=GROUP), :] = v
    return scratch[...]


def means_kernel(weight, table, field, goal, means, jacobian, self_block, cell_diag, out, scratch):
    steps = means.shape[1]

    def step(b, u):
        lanes = lanes_of(b)
        total = []
        for a in range(NV):
            v = field[a, :, lanes]
            fine = goal[a, :, lanes] - weight * (3.0 * v - 4.0 * earlier(v, 1) + earlier(v, 2))
            total.append(mean_rows(fine, scratch.at[u, a], steps) - cell_diag[pl.ds(a, 1), lanes] * means[a, :, lanes])
        total = own_part(total, b, means, table, jacobian, self_block)
        for a in range(NV):
            out[a, :, lanes] = total[a]

    each_block(table.shape[1], step)


def beside_part(table, part, rim, rim_jacobian, out):
    def step(b, u):
        lanes = lanes_of(b)
        total = rim_part(1, [part[a, :, lanes] for a in range(NV)], b, rim, table, rim_jacobian)
        for a in range(NV):
            out[a, :, lanes] = total[a]

    each_block(table.shape[1], step)


def step_of(listed, h, a, field, part, points):
    lanes = lanes_of(listed[h])
    return field[a, :, lanes] + points[pl.ds(a, 1), lanes] * part[a, :, lanes]


def message_kernel(table, listed, field, part, rim, rim_jacobian, points, out, message):
    beside_part(table, part, rim, rim_jacobian, out)
    for h in range(listed.shape[0]):
        for a in range(NV):
            message[h, a] = step_of(listed, h, a, field, out, points)


def first_message_kernel(
    table, listed, field, part, rim, rim_jacobian, points, coarse_points, tail, out, message
):
    beside_part(table, part, rim, rim_jacobian, out)
    steps = field.shape[1]
    behind = NV * steps
    for h in range(listed.shape[0]):
        block = listed[h]
        lanes = lanes_of(block)
        for a in range(NV):
            message[h, pl.ds(a * steps, steps), :] = step_of(listed, h, a, field, out, points)
            message[h, pl.ds(behind + NV * a, NV), :] = rim_jacobian[0, a, :, lanes]
        message[h, pl.ds(behind + NV * NV, NV), :] = points[:, lanes]
        message[h, pl.ds(behind + NV * NV + NV, NV), :] = coarse_points[:, lanes]
        named = jnp.full((1, BLK), table[0, block], jnp.int32)
        message[h, pl.ds(behind + NV * NV + 2 * NV, 1), :] = named.astype(jnp.float32)


def means_message_kernel(table, listed, field, part, rim, rim_jacobian, points, out, message, scratch):
    beside_part(table, part, rim, rim_jacobian, out)
    steps = field.shape[1]
    coarse = steps // GROUP
    for h in range(listed.shape[0]):
        for a in range(NV):
            v = step_of(listed, h, a, field, out, points)
            message[h, a, pl.ds(0, coarse), :] = mean_rows(v, scratch.at[h % UNROLL, a], coarse)
            message[h, a, pl.ds(coarse, 2), :] = v[steps - 2 :]


def scaled_message_kernel(table, listed, part, rim, rim_jacobian, points, out, message):
    beside_part(table, part, rim, rim_jacobian, out)
    for h in range(listed.shape[0]):
        lanes = lanes_of(listed[h])
        for a in range(NV):
            message[h, a] = points[pl.ds(a, 1), lanes] * out[a, :, lanes]


def corrected_message_kernel(table, listed, field, part, rim, fine, rim_jacobian, points, out, message, scratch):
    beside_part(table, part, rim, rim_jacobian, out)
    for h in range(listed.shape[0]):
        for a in range(NV):
            v = step_of(listed, h, a, field, out, points)
            message[h, a] = fine[a, :, lanes_of(listed[h])] + spread_rows(v, scratch.at[h % UNROLL, a])


class Partner:
    def __init__(self, ref, steps, level):
        self.ref, self.behind, self.level = ref, NV * steps, level

    def row(self, h, r):
        return self.ref[h, pl.ds(self.behind + r, 1), :]

    def coupling(self, h):
        return lambda a, j: self.row(h, NV * a + j)

    def point(self, h, a):
        return self.row(h, NV * (NV + self.level) + a)


def index_kernel(steps, message, next_message, index):
    partner = Partner(message, steps, 0)
    for h in range(index.shape[0]):
        index[h] = jnp.max(partner.row(h, NV * (NV + 2))).astype(jnp.int32)


def own_share(index, h, faces, partner):
    block = index[h]
    zero = [jnp.zeros(faces.shape[2:], jnp.float32)] * NV
    total = coupled(zero, partner.coupling(h), [faces[block, j] for j in range(NV)])
    return [partner.point(h, a) * total[a] for a in range(NV)]


def rim_kernel(steps, level, index, faces, message, first_message, out):
    partner = Partner(first_message, steps, level)

    def step(h, u):
        share = own_share(index, h, faces, partner)
        for a in range(NV):
            if len(message.shape) == 3:
                out[h, a] = message[h, pl.ds(a * steps, steps), :] + share[a]
            else:
                out[h, a] = message[h, a] + share[a]

    each_block(index.shape[0], step)


def means_rim_kernel(steps, index, faces, message, first_message, out, last_out, scratch):
    partner = Partner(first_message, steps, 0)
    coarse = out.shape[2]

    def step(h, u):
        share = own_share(index, h, faces, partner)
        for a in range(NV):
            out[h, a] = message[h, a, pl.ds(0, coarse), :] + mean_rows(share[a], scratch.at[u, a], coarse)
            last_out[h, a] = message[h, a, pl.ds(coarse, 2), :] + share[a][steps - 2 :]

    each_block(index.shape[0], step)


def corrected_rim_kernel(steps, index, faces, message, first_message, out, scratch):
    partner = Partner(first_message, steps, 1)

    def step(h, u):
        share = own_share(index, h, faces, partner)
        for a in range(NV):
            out[h, a] = message[h, a] + spread_rows(share[a], scratch.at[u, a])

    each_block(index.shape[0], step)


def padded(rows, count):
    pad = count - rows.shape[0]
    return jnp.concatenate([rows, jnp.zeros((pad, BLK), jnp.float32)], axis=0) if pad > 0 else rows


def spread_tail(rows):
    return jnp.concatenate([jnp.broadcast_to(rows[i : i + 1], (GROUP, BLK)) for i in range(2)], axis=0)


def rim_tail(h, a, tail, cells, partner, spread):
    rows = tail[a, :, pl.ds(pl.multiple_of(cells + h * BLK, BLK), BLK)]
    rows = partner.point(h, a) * rows
    return spread_tail(rows) if spread else rows


def finish_kernel(steps, level, spread, rim, tail, first_message, rim_out):
    partner = Partner(first_message, steps, level)
    cells = tail.shape[2] - rim.shape[0] * BLK

    def step(h, u):
        for a in range(NV):
            rows = rim_tail(h, a, tail, cells, partner, spread)
            rim_out[h, a] = rim[h, a] - padded(rows, rim.shape[2])

    each_block(rim.shape[0], step)


def rest_part(b, part, rim, table, rim_jacobian):
    lanes = lanes_of(b)
    return rim_part(0, [part[a, :, lanes] for a in range(NV)], b, rim, table, rim_jacobian)


def sweep_kernel(weights, table, field, part, rim, rim_jacobian, points, out, *tail_out):
    def step(b, u):
        lanes = lanes_of(b)
        total = rest_part(b, part, rim, table, rim_jacobian)
        for a in range(NV):
            out[a, :, lanes] = field[a, :, lanes] + points[pl.ds(a, 1), lanes] * total[a]

    each_block(table.shape[1], step)
    if tail_out:
        send_tail(weights, out, rim, tail_out[0])


def first_correction_kernel(weights, table, part, rim, last_rows, rim_jacobian, points, out, defect_out, *tail_out):
    def step(b, u):
        lanes = lanes_of(b)
        total = rest_part(b, part, rim, table, rim_jacobian)
        for a in range(NV):
            defect_out[a, :, lanes] = total[a]
            out[a, :, lanes] = points[pl.ds(a, 1), lanes] * total[a]

    each_block(table.shape[1], step)
    if tail_out:
        send_tail(weights, out, last_rows, tail_out[0])


def corrected_kernel(weights, table, field, part, rim, fine, rim_jacobian, points, out, *refs):
    scratch = refs[-1]

    def step(b, u):
        lanes = lanes_of(b)
        total = rest_part(b, part, rim, table, rim_jacobian)
        for a in range(NV):
            v = field[a, :, lanes] + points[pl.ds(a, 1), lanes] * total[a]
            out[a, :, lanes] = fine[a, :, lanes] + spread_rows(v, scratch.at[u, a])

    each_block(table.shape[1], step)
    if len(refs) > 1:
        send_tail(weights, out, rim, refs[0])


def last_own_kernel(weight, table, field, goal, jacobian, self_block, cell_diag, out, updated, sem):
    copy = pltpu.make_async_copy(field, updated, sem)
    copy.start()
    own_kernel(weight, table, field, goal, jacobian, self_block, cell_diag, out)
    copy.wait()


def last_rim_kernel(steps, index, faces, message, tail, first_message, out):
    rim_kernel(steps, 0, index, faces, message, first_message, out)
    partner = Partner(first_message, steps, 0)
    cells = tail.shape[2] - index.shape[0] * BLK

    def step(h, u):
        for a in range(NV):
            out[h, a, pl.ds(0, 2), :] = out[h, a, pl.ds(0, 2), :] - rim_tail(h, a, tail, cells, partner, False)

    each_block(index.shape[0], step)


def residual_kernel(table, part, rim, tail, rim_jacobian, out, held, sems):
    blocks = table.shape[1]

    def send(b):
        lanes = lanes_of(b)
        return pltpu.make_async_copy(held.at[:, :, lanes], out.at[:, :, lanes], sems.at[b])

    def step(b, u):
        lanes = lanes_of(b)
        total = rest_part(b, part, rim, table, rim_jacobian)
        for a in range(NV):
            held[a, :, lanes] = total[a]
            add_rows(held, a, lanes, -tail[a, :, lanes])
        send(b).start()

    each_block(blocks, step)
    each_block(blocks, lambda b, u: send(b).wait())


def earlier_steps(b, tail, table, rim_jacobian, partner, spread):
    lanes = lanes_of(b)
    total = [-tail[a, :, lanes] for a in range(NV)]
    if partner is None:
        return total
    if spread:
        total = [padded(rows, 2 * GROUP) for rows in total]
    cells = table.shape[1] * BLK
    block = table[0, b]
    values = [-rim_tail(block, j, tail, cells, partner, spread) for j in range(NV)]
    return coupled(total, lambda a, j: rim_jacobian[0, a, pl.ds(j, 1), lanes], values)


def add_rows(out, a, lanes, rows):
    first = pl.ds(0, rows.shape[0])
    out[a, first, lanes] = out[a, first, lanes] + rows


def partner_of(first_message, steps, level):
    return None if level is None else Partner(first_message, steps, level)


def finish_sweep_kernel(
    steps, level, spread, spread_out, table, listed, field, tail, first_message, rim_jacobian, points, out, faces_out
):
    partner = partner_of(first_message, steps, level)

    def step(b, u):
        lanes = lanes_of(b)
        total = earlier_steps(b, tail, table, rim_jacobian, partner, spread)
        for a in range(NV):
            rows = points[pl.ds(a, 1), lanes] * total[a]
            add_rows(out, a, lanes, spread_tail(rows) if spread_out else rows)

    each_block(table.shape[1], step)
    pick_faces(listed, out, faces_out)


def finish_smoothed_kernel(
    steps, level, table, listed, field, tail, first_message, rim_jacobian, points, out, means_out, faces_out, scratch
):
    partner = partner_of(first_message, steps, level)

    def step(b, u):
        lanes = lanes_of(b)
        total = earlier_steps(b, tail, table, rim_jacobian, partner, False)
        for a in range(NV):
            add_rows(out, a, lanes, points[pl.ds(a, 1), lanes] * total[a])
            means_out[a, :, lanes] = mean_rows(out[a, :, lanes], scratch.at[u, a], means_out.shape[1])

    each_block(table.shape[1], step)
    pick_faces(listed, means_out, faces_out)


def finish_correction_kernel(
    steps, level, table, listed, field, defect, tail, first_message, rim_jacobian, points, out, defect_out, faces_out
):
    partner = partner_of(first_message, steps, level)

    def step(b, u):
        lanes = lanes_of(b)
        total = earlier_steps(b, tail, table, rim_jacobian, partner, False)
        for a in range(NV):
            add_rows(defect_out, a, lanes, total[a])
            add_rows(out, a, lanes, points[pl.ds(a, 1), lanes] * total[a])

    each_block(table.shape[1], step)
    pick_faces(listed, out, faces_out)


def neighbour_pairs(first):
    pairs = [(i, i + 1) for i in range(first, lax.axis_size("space") - 1, 2)]
    return pairs + [(j, i) for i, j in pairs]


def over_chips(message):
    return lax.ppermute(message, "space", neighbour_pairs(1))


def on_chip(faces):
    return lax.ppermute(faces, "space", neighbour_pairs(0))


def to_later(tail):
    periods = lax.axis_size("tm")
    return lax.ppermute(tail, "tm", [(i, (i + 1) % periods) for i in range(periods)])


def body(iterate, right_side, jacobian, self_block, cell_diag, neighbours, face_list):
    steps, cells = iterate.shape[0], iterate.shape[2]
    blocks, faces = cells // BLK, face_list.shape[0]
    coarse = steps // GROUP
    per_slot = 2 * blocks * NV * NV * BLK

    whole = lambda n: shape(NV, n, cells)
    face = lambda n: shape(faces, NV, n, BLK)
    spare = lambda more, n: shape(faces + more, NV, n, BLK)
    rows_scratch = [pltpu.VMEM((UNROLL, NV, steps, BLK), jnp.float32)]
    bind = functools.partial
    plain = lambda rows: rows

    goal = jnp.transpose(right_side, (1, 0, 2))
    jacobian = jnp.transpose(jacobian, (1, 2, 0, 3))
    table, listed, start, sent = pl.pallas_call(
        first_kernel,
        out_shape=[
            pltpu.SMEM((K, blocks), jnp.int32), pltpu.SMEM((faces,), jnp.int32),
            pltpu.VMEM((NV, steps, cells), jnp.float32), pltpu.VMEM(face(steps).shape, jnp.float32),
        ],
        in_specs=[IN_HBM] * 3,
        out_specs=[IN_SMEM] * 2 + [IN_VMEM] * 2,
        scratch_shapes=[
            pltpu.SMEM((K, blocks), jnp.int32), pltpu.SMEM((faces,), jnp.int32), pltpu.SemaphoreType.DMA((3,)),
        ],
        compiler_params=pltpu.CompilerParams(vmem_limit_bytes=SCRATCH_BYTES),
        cost_estimate=NOTHING,
        name="iterate_and_tables",
    )(*[in_hbm(x) for x in (jnp.transpose(neighbours), face_list, jnp.transpose(iterate, (1, 0, 2)))])
    tables = [table, listed]
    rim = over_chips(sent)
    beside = on_chip(sent)
    arguments = [in_hbm(x) for x in (cell_diag, jacobian, self_block, goal)]
    outs = [shape(*x.shape) for x in arguments] + [shape(NV, cells)] * 2 + [shape(2, NV, NV, cells)]
    cell_diag, jacobian, self_block, goal, fine_points, coarse_points, rim_jacobian = pl.pallas_call(
        arguments_kernel,
        out_shape=[pltpu.VMEM(x.shape, jnp.float32) for x in outs],
        in_specs=[IN_SMEM] + [IN_HBM] * len(arguments),
        out_specs=[IN_VMEM] * len(outs),
        scratch_shapes=[pltpu.SemaphoreType.DMA((len(arguments),))],
        compiler_params=pltpu.CompilerParams(vmem_limit_bytes=SCRATCH_BYTES),
        cost_estimate=NOTHING,
        name="arguments",
    )(listed, *arguments)

    def own(weight, n, field, target):
        return call(
            bind(own_kernel, weight), "own_part", [table], [field, target, jacobian, self_block, cell_diag],
            [whole(n)], 5 * per_slot * n,
        )[0]

    ahead = coarse >= 4
    tail_shape = shape(NV, 2, cells + faces * BLK)

    state = start
    first_tail = call(
        bind(tail_kernel, (time_weight, False, None, None)), "tail", [], [state], [shape(NV, 2, cells)]
    )[0]
    tail = to_later(first_tail)
    part = own(time_weight, steps, state, goal)
    part, message = call(
        first_message_kernel, "first_message", tables,
        [state, part, beside, rim_jacobian, fine_points, coarse_points, tail],
        [whole(steps), shape(faces, NV * steps + NV * (NV + 3), BLK)], per_slot * steps,
    )
    first_message = over_chips(message)
    message = first_message
    earlier_sent = sent

    def plan(weights, tail, level, spread=False):
        def ready(rim):
            if ahead or level is None:
                return rim, level
            return call(
                bind(finish_kernel, steps, level, spread), "finish_rim", [], [rim, tail, first_message],
                [shape(*rim.shape)],
            )[0], None

        return ready

    def sweep(kernel, name, arrays, behind, outs, rim, weights, tail, level, spread, finisher, scratch=(), tail_rim=None):
        rim, level = plan(weights, tail, level, spread)(rim)
        sources = rim if tail_rim is None else tail_rim
        extra = [] if tail_rim is None else [tail_rim]
        results = call(
            bind(kernel, weights), name, [table], arrays + [rim] + extra + behind,
            outs + [tail_shape] * ahead, per_slot * steps, scratch,
        )
        if ahead:
            next_tail = to_later(results[-1])
            results = results[:-1]
        finished = finisher(results, tail, level)
        if not ahead:
            next_tail = to_later(call(bind(tail_kernel, weights), "tail", [], [finished[0], sources], [tail_shape])[0])
        return finished, next_tail, rim

    def finish_with(points, n, spread=False, spread_out=False):
        def finisher(results, tail, level):
            return call(
                bind(finish_sweep_kernel, steps, level, spread, spread_out), "finish_sweep", tables,
                [results[0], tail, points if level is None else first_message, rim_jacobian, points],
                [whole(n), face(n)], 0, (), None, 1,
            )

        return finisher

    fine_weights = (time_weight, False, time_weight, False)
    (state, sent), tail, rim = sweep(
        sweep_kernel, "first_sweep", [state, part], [rim_jacobian, fine_points], [whole(steps)], rim, fine_weights,
        tail, None, False, finish_with(fine_points, steps),
    )
    beside = on_chip(sent)
    part = own(time_weight, steps, state, goal)
    part, next_message = call(
        means_message_kernel, "message_of_means", tables, [state, part, beside, rim_jacobian, fine_points],
        [whole(steps), face(coarse + 2)], per_slot * steps, rows_scratch,
    )
    index = pl.pallas_call(
        bind(index_kernel, steps), out_shape=pltpu.SMEM((faces,), jnp.int32), in_specs=[IN_VMEM] * 2,
        out_specs=IN_SMEM, name="coupled_faces", cost_estimate=NOTHING,
        compiler_params=pltpu.CompilerParams(vmem_limit_bytes=SCRATCH_BYTES),
    )(*[pltpu.with_memory_space_constraint(x, pltpu.VMEM) for x in (first_message, next_message)])
    next_message = over_chips(next_message)
    rim = call(
        bind(rim_kernel, steps, 0), "rim", [index], [earlier_sent, message, first_message], [face(steps)],
        per_slot * steps // 2,
    )[0]
    message, earlier_sent = next_message, sent

    def finish_smoothed(results, tail, level):
        return call(
            bind(finish_smoothed_kernel, steps, level), "finish_and_means", tables,
            [results[0], tail, first_message, rim_jacobian, fine_points],
            [whole(steps), whole(coarse), face(coarse)], 0, rows_scratch, None, 1,
        )

    (state, means, sent), tail, rim = sweep(
        sweep_kernel, "sweep", [state, part], [rim_jacobian, fine_points], [whole(steps)], rim,
        (time_weight, True, time_weight, True), tail, 0, False, finish_smoothed,
    )

    beside = on_chip(sent)
    part = call(
        bind(means_kernel, time_weight), "own_part_of_means", [table],
        [state, goal, means, jacobian, self_block, cell_diag], [whole(coarse)], 5 * per_slot * coarse, rows_scratch,
    )[0]
    part, next_message = call(
        scaled_message_kernel, "message_of_correction", tables, [part, beside, rim_jacobian, coarse_points],
        [whole(coarse), spare(faces, coarse)], per_slot * coarse,
    )
    next_message = over_chips(next_message)
    rim, last_rows = call(
        bind(means_rim_kernel, steps), "rim_of_means", [index], [earlier_sent, message, first_message],
        [face(coarse), face(2)], per_slot * steps // 2, rows_scratch,
    )
    message, earlier_sent = next_message, sent

    def finish_correction(results, tail, level):
        return call(
            bind(finish_correction_kernel, steps, level), "finish_correction", tables,
            [*results, tail, first_message, rim_jacobian, coarse_points],
            [whole(coarse), whole(coarse), face(coarse)], 0, (), None, 2,
        )

    (correction, defect, sent), tail, rim = sweep(
        first_correction_kernel, "first_correction", [part], [rim_jacobian, coarse_points],
        [whole(coarse), whole(coarse)], rim, (coarse_weight, False, time_weight, True), tail, 0, False,
        finish_correction, (), last_rows,
    )

    for sweep_no in range(NUC - 1):
        beside = on_chip(sent)
        part = own(coarse_weight, coarse, correction, defect)
        last = sweep_no == NUC - 2
        if last:
            part, next_message = call(
                corrected_message_kernel, "message_of_corrected", tables,
                [correction, part, beside, state, rim_jacobian, coarse_points],
                [whole(coarse), spare(1, steps)], per_slot * coarse, rows_scratch,
            )
        else:
            part, next_message = call(
                message_kernel, "message_of_coarse", tables, [correction, part, beside, rim_jacobian, coarse_points],
                [whole(coarse), spare(faces, coarse)], per_slot * coarse,
            )
        next_message = over_chips(next_message)
        rim = call(
            bind(rim_kernel, steps, 1), "rim_of_coarse", [index], [earlier_sent, message, first_message],
            [face(coarse)], per_slot * coarse // 2,
        )[0]
        message, earlier_sent = next_message, sent
        if last:
            (state, sent), tail, rim = sweep(
                corrected_kernel, "corrected", [correction, part], [state, rim_jacobian, coarse_points],
                [whole(steps)], rim, (time_weight, False, coarse_weight, False), tail, 1, False,
                finish_with(coarse_points, steps, False, True), rows_scratch,
            )
        else:
            (correction, sent), tail, rim = sweep(
                sweep_kernel, "coarse_sweep", [correction, part], [rim_jacobian, coarse_points], [whole(coarse)],
                rim, (coarse_weight, False, coarse_weight, False), tail, 1, False, finish_with(coarse_points, coarse),
            )

    for sweep_no in range(NU2 + 1):
        beside = on_chip(sent)
        if sweep_no == NU2:
            break
        part = own(time_weight, steps, state, goal)
        part, next_message = call(
            message_kernel, "message", tables, [state, part, beside, rim_jacobian, fine_points],
            [whole(steps), spare(1, steps)], per_slot * steps,
        )
        next_message = over_chips(next_message)
        if sweep_no == 0:
            rim = call(
                bind(corrected_rim_kernel, steps), "rim_of_corrected", [index],
                [earlier_sent, message, first_message], [face(steps)], per_slot * coarse // 2, rows_scratch,
            )[0]
        else:
            rim = call(
                bind(rim_kernel, steps, 0), "rim", [index], [earlier_sent, message, first_message],
                [face(steps)], per_slot * steps // 2,
            )[0]
        message, earlier_sent = next_message, sent
        spread = sweep_no == 0
        (state, sent), tail, rim = sweep(
            sweep_kernel, "sweep", [state, part], [rim_jacobian, fine_points], [whole(steps)], rim, fine_weights,
            tail, 1 if spread else 0, spread, finish_with(fine_points, steps, spread),
        )
    part, updated = call(
        bind(last_own_kernel, time_weight), "last_own_part", [table],
        [state, goal, jacobian, self_block, cell_diag], [whole(steps)] * 2, 5 * per_slot * steps,
        [pltpu.SemaphoreType.DMA], [IN_VMEM, IN_HBM],
    )
    part = call(beside_part, "beside_part", [table], [part, beside, rim_jacobian], [whole(steps)], per_slot * steps)[0]
    rim = call(
        bind(last_rim_kernel, steps), "rim", [index], [earlier_sent, message, tail, first_message], [face(steps)],
        per_slot * steps // 2,
    )[0]
    residual = call(
        residual_kernel, "residual", [table], [part, rim, tail, rim_jacobian], [whole(steps)], per_slot * steps,
        [pltpu.VMEM((NV, steps, cells), jnp.float32), pltpu.SemaphoreType.DMA((blocks,))], [IN_HBM],
    )[0]
    return jnp.transpose(updated, (1, 0, 2)), jnp.transpose(residual, (1, 0, 2))


def solution(mesh):
    in_specs = (
        P("tm", None, "space"),
        P("tm", None, "space"),
        P(None, None, None, "space"),
        P(None, None, "space"),
        P(None, "space"),
        P("space", None),
        P("space"),
    )
    out_specs = (P("tm", None, "space"), P("tm", None, "space"))
    return jax.shard_map(body, mesh=mesh, in_specs=in_specs, out_specs=out_specs, check_vma=False)
```

```python
import functools

import jax
import jax.numpy as jnp
from jax import lax
from jax.experimental import pallas as pl
from jax.experimental.pallas import tpu as pltpu
from jax.sharding import PartitionSpec as P

NV = 5
BLK = 128
K = 6
NU1 = 2
NU2 = 2
NUC = 4
GROUP = 4

time_weight = 0.5
coarse_weight = time_weight / GROUP
damping = 0.7

UNROLL = 8
SCRATCH_BYTES = 4 << 20
IN_VMEM = pl.BlockSpec(memory_space=pltpu.VMEM)
NOTHING = pl.CostEstimate(flops=1, bytes_accessed=1, transcendentals=0)
LONG = pl.CostEstimate(flops=0, bytes_accessed=100 << 20, transcendentals=0)
IN_HBM = pl.BlockSpec(memory_space=pltpu.HBM)
IN_SMEM = pl.BlockSpec(memory_space=pltpu.SMEM)


def call(kernel, name, tables, arrays, outs, flops=0, scratch=(), out_specs=None, in_place=0):
    arrays = [pltpu.with_memory_space_constraint(a, pltpu.VMEM) for a in arrays]
    size = 4 * (sum(a.size for a in arrays) + sum(o.size for o in outs))
    return pl.pallas_call(
        kernel,
        out_shape=[
            o if out_specs and out_specs[i] is IN_HBM else pltpu.VMEM(o.shape, o.dtype) for i, o in enumerate(outs)
        ],
        in_specs=[IN_SMEM] * len(tables) + [IN_VMEM] * len(arrays),
        out_specs=out_specs or [IN_VMEM] * len(outs),
        scratch_shapes=scratch,
        input_output_aliases={len(tables) + i: i for i in range(in_place)},
        cost_estimate=LONG if name.startswith('rim') else NOTHING,
        compiler_params=pltpu.CompilerParams(vmem_limit_bytes=SCRATCH_BYTES),
        name=name,
    )(*tables, *arrays)


def in_hbm(array):
    return pltpu.with_memory_space_constraint(array, pltpu.HBM)


def shape(*dims):
    return jax.ShapeDtypeStruct(dims, jnp.float32)


def lanes_of(b):
    return pl.ds(pl.multiple_of(b * BLK, BLK), BLK)


def cross_slot():
    return lax.rem(lax.axis_index("space"), 2)


def each_block(count, step):
    unroll = UNROLL if count % UNROLL == 0 else 1

    def steps(i, carry):
        for u in range(unroll):
            step(i * unroll + u, u)
        return carry

    lax.fori_loop(0, count // unroll, steps, 0)


def first_kernel(*refs):
    sources, (table, listed, *held, faces_out, near, named, sems) = refs[:7], refs[7:]
    copies = [pltpu.make_async_copy(x, y, sems.at[i]) for i, (x, y) in enumerate(zip(sources, [near, named, *held]))]
    for copy in copies:
        copy.start()
    slot = cross_slot()
    slots, blocks = near.shape
    faces = named.shape[0]
    copies[0].wait()

    def step(b, carry):
        table[0, b] = near[slot, b] - (blocks + faces * slot)
        table[1, b] = near[1 - slot, b] - (blocks + faces * (1 - slot))
        for k in range(2, slots):
            table[k, b] = near[k, b]
        return carry

    lax.fori_loop(0, blocks, step, 0)
    copies[1].wait()
    for h in range(faces):
        listed[h] = named[h]
    copies[2].wait()
    pick_faces(listed, held[0], faces_out)
    for copy in copies[3:]:
        copy.wait()


def derived_kernel(listed, cell_diag, jacobian, fine_out, coarse_out, out):
    lower_crosses = cross_slot() == 0
    fine_out[...] = damping / (3.0 * time_weight + cell_diag[...])
    coarse_out[...] = damping / (3.0 * coarse_weight + cell_diag[...])
    for a in range(NV):
        for j in range(NV):
            lower, upper = jacobian[a, j, pl.ds(0, 1), :], jacobian[a, j, pl.ds(1, 1), :]
            out[0, a, pl.ds(j, 1), :] = jnp.where(lower_crosses, lower, upper)
            out[1, a, pl.ds(j, 1), :] = jnp.where(lower_crosses, upper, lower)


def coupled(total, coupling, values):
    for j in range(NV):
        for a in range(NV):
            total[a] = total[a] - coupling(a, j) * values[j]
    return total


def earlier(v, steps):
    if v.shape[0] <= steps:
        return jnp.zeros_like(v)
    return jnp.concatenate([jnp.zeros((steps, BLK), jnp.float32), v[: v.shape[0] - steps]], axis=0)


def own_part(total, b, field, table, jacobian, self_block):
    lanes = lanes_of(b)
    v = [field[j, :, lanes] for j in range(NV)]
    for a in range(NV):
        for j in range(NV):
            if j != a:
                total[a] = total[a] - self_block[a, pl.ds(j, 1), lanes] * v[j]
    for slot in range(2, K):
        there = lanes_of(table[slot, b])
        row = pl.ds(slot, 1)
        total = coupled(total, lambda a, j: jacobian[a, j, row, lanes], [field[j, :, there] for j in range(NV)])
    return total


def rim_part(side, total, b, rim, table, rim_jacobian):
    block, lanes = table[side, b], lanes_of(b)
    coupling = lambda a, j: rim_jacobian[side, a, pl.ds(j, 1), lanes]
    return coupled(total, coupling, [rim[block, j] for j in range(NV)])


def pick_faces(listed, field, faces_out):
    for h in range(listed.shape[0]):
        lanes = lanes_of(listed[h])
        for a in range(NV):
            faces_out[h, a] = field[a, :, lanes]


def tail_rows(last_two, weight, mean):
    last = last_two[1:]
    if mean:
        return jnp.concatenate([(weight / GROUP) * (last_two[:1] - 3.0 * last), jnp.zeros_like(last)], axis=0)
    return weight * jnp.concatenate([last_two[:1] - 4.0 * last, last], axis=0)


def send_tail(weights, field, rim, tail_out):
    steps, cells = field.shape[1:]
    weight, mean, rim_weight, rim_mean = weights
    for a in range(NV):
        before, last = field[a, pl.ds(steps - 2, 1), :], field[a, pl.ds(steps - 1, 1), :]
        if mean:
            tail_out[a, pl.ds(0, 1), pl.ds(0, cells)] = (weight / GROUP) * (before - 3.0 * last)
            tail_out[a, pl.ds(1, 1), pl.ds(0, cells)] = jnp.zeros_like(last)
        else:
            tail_out[a, pl.ds(0, 1), pl.ds(0, cells)] = weight * (before - 4.0 * last)
            tail_out[a, pl.ds(1, 1), pl.ds(0, cells)] = weight * last
    if rim is not None:
        for h in range((tail_out.shape[2] - cells) // BLK):
            for a in range(NV):
                rows = tail_rows(rim[h, a, pl.ds(rim.shape[2] - 2, 2), :], rim_weight, rim_mean)
                tail_out[a, :, pl.ds(cells + h * BLK, BLK)] = rows


def tail_kernel(weights, field, *refs):
    send_tail(weights, field, refs[0] if len(refs) > 1 else None, refs[-1])


def own_kernel(weight, table, field, goal, jacobian, self_block, cell_diag, out):
    def step(b, u):
        lanes = lanes_of(b)
        total = []
        for a in range(NV):
            v = field[a, :, lanes]
            point = 3.0 * weight + cell_diag[pl.ds(a, 1), lanes]
            timed = weight * (earlier(v, 2) - 4.0 * earlier(v, 1))
            total.append(goal[a, :, lanes] - point * v - timed)
        total = own_part(total, b, field, table, jacobian, self_block)
        for a in range(NV):
            out[a, :, lanes] = total[a]

    each_block(table.shape[1], step)


def mean_rows(v, scratch, steps):
    scratch[...] = v
    return sum(scratch[pl.ds(i, steps, stride=GROUP), :] for i in range(GROUP)) * (1.0 / GROUP)


def spread_rows(v, scratch):
    for i in range(GROUP):
        scratch[pl.ds(i, v.shape[0], stride=GROUP), :] = v
    return scratch[...]


def means_kernel(weight, table, field, goal, means, jacobian, self_block, cell_diag, out, scratch):
    steps = means.shape[1]

    def step(b, u):
        lanes = lanes_of(b)
        total = []
        for a in range(NV):
            v = field[a, :, lanes]
            fine = goal[a, :, lanes] - weight * (3.0 * v - 4.0 * earlier(v, 1) + earlier(v, 2))
            total.append(mean_rows(fine, scratch.at[u, a], steps) - cell_diag[pl.ds(a, 1), lanes] * means[a, :, lanes])
        total = own_part(total, b, means, table, jacobian, self_block)
        for a in range(NV):
            out[a, :, lanes] = total[a]

    each_block(table.shape[1], step)


def beside_part(table, part, rim, rim_jacobian, out):
    def step(b, u):
        lanes = lanes_of(b)
        total = rim_part(1, [part[a, :, lanes] for a in range(NV)], b, rim, table, rim_jacobian)
        for a in range(NV):
            out[a, :, lanes] = total[a]

    each_block(table.shape[1], step)


def step_of(listed, h, a, field, part, points):
    lanes = lanes_of(listed[h])
    return field[a, :, lanes] + points[pl.ds(a, 1), lanes] * part[a, :, lanes]


def message_kernel(table, listed, field, part, rim, rim_jacobian, points, out, message):
    beside_part(table, part, rim, rim_jacobian, out)
    for h in range(listed.shape[0]):
        for a in range(NV):
            message[h, a] = step_of(listed, h, a, field, out, points)


def first_message_kernel(
    table, listed, field, part, rim, rim_jacobian, points, coarse_points, out, message
):
    beside_part(table, part, rim, rim_jacobian, out)
    steps = field.shape[1]
    behind = NV * steps
    for h in range(listed.shape[0]):
        block = listed[h]
        lanes = lanes_of(block)
        for a in range(NV):
            message[h, pl.ds(a * steps, steps), :] = step_of(listed, h, a, field, out, points)
            message[h, pl.ds(behind + NV * a, NV), :] = rim_jacobian[0, a, :, lanes]
        message[h, pl.ds(behind + NV * NV, NV), :] = points[:, lanes]
        message[h, pl.ds(behind + NV * NV + NV, NV), :] = coarse_points[:, lanes]
        named = jnp.full((1, BLK), table[0, block], jnp.int32)
        message[h, pl.ds(behind + NV * NV + 2 * NV, 1), :] = named.astype(jnp.float32)


def means_message_kernel(table, listed, field, part, rim, rim_jacobian, points, out, message, scratch):
    beside_part(table, part, rim, rim_jacobian, out)
    steps = field.shape[1]
    coarse = steps // GROUP
    for h in range(listed.shape[0]):
        for a in range(NV):
            v = step_of(listed, h, a, field, out, points)
            message[h, a, pl.ds(0, coarse), :] = mean_rows(v, scratch.at[h % UNROLL, a], coarse)
            message[h, a, pl.ds(coarse, 2), :] = v[steps - 2 :]


def scaled_message_kernel(table, listed, part, rim, rim_jacobian, points, out, message):
    beside_part(table, part, rim, rim_jacobian, out)
    for h in range(listed.shape[0]):
        lanes = lanes_of(listed[h])
        for a in range(NV):
            message[h, a] = points[pl.ds(a, 1), lanes] * out[a, :, lanes]


def corrected_message_kernel(table, listed, field, part, rim, fine, rim_jacobian, points, out, message, scratch):
    beside_part(table, part, rim, rim_jacobian, out)
    for h in range(listed.shape[0]):
        for a in range(NV):
            v = step_of(listed, h, a, field, out, points)
            message[h, a] = fine[a, :, lanes_of(listed[h])] + spread_rows(v, scratch.at[h % UNROLL, a])


class Partner:
    def __init__(self, ref, steps, level):
        self.ref, self.behind, self.level = ref, NV * steps, level

    def row(self, h, r):
        return self.ref[h, pl.ds(self.behind + r, 1), :]

    def coupling(self, h):
        return lambda a, j: self.row(h, NV * a + j)

    def point(self, h, a):
        return self.row(h, NV * (NV + self.level) + a)


def index_kernel(steps, message, next_message, index):
    partner = Partner(message, steps, 0)
    for h in range(index.shape[0]):
        index[h] = jnp.max(partner.row(h, NV * (NV + 2))).astype(jnp.int32)


def own_share(index, h, faces, partner):
    block = index[h]
    zero = [jnp.zeros(faces.shape[2:], jnp.float32)] * NV
    total = coupled(zero, partner.coupling(h), [faces[block, j] for j in range(NV)])
    return [partner.point(h, a) * total[a] for a in range(NV)]


def rim_kernel(steps, level, index, faces, message, first_message, out):
    partner = Partner(first_message, steps, level)

    def step(h, u):
        share = own_share(index, h, faces, partner)
        for a in range(NV):
            if len(message.shape) == 3:
                out[h, a] = message[h, pl.ds(a * steps, steps), :] + share[a]
            else:
                out[h, a] = message[h, a] + share[a]

    each_block(index.shape[0], step)


def means_rim_kernel(steps, index, faces, message, first_message, out, last_out, scratch):
    partner = Partner(first_message, steps, 0)
    coarse = out.shape[2]

    def step(h, u):
        share = own_share(index, h, faces, partner)
        for a in range(NV):
            out[h, a] = message[h, a, pl.ds(0, coarse), :] + mean_rows(share[a], scratch.at[u, a], coarse)
            last_out[h, a] = message[h, a, pl.ds(coarse, 2), :] + share[a][steps - 2 :]

    each_block(index.shape[0], step)


def corrected_rim_kernel(steps, index, faces, message, first_message, out, scratch):
    partner = Partner(first_message, steps, 1)

    def step(h, u):
        share = own_share(index, h, faces, partner)
        for a in range(NV):
            out[h, a] = message[h, a] + spread_rows(share[a], scratch.at[u, a])

    each_block(index.shape[0], step)


def padded(rows, count):
    pad = count - rows.shape[0]
    return jnp.concatenate([rows, jnp.zeros((pad, BLK), jnp.float32)], axis=0) if pad > 0 else rows


def spread_tail(rows):
    return jnp.concatenate([jnp.broadcast_to(rows[i : i + 1], (GROUP, BLK)) for i in range(2)], axis=0)


def rim_tail(h, a, tail, cells, partner, spread):
    rows = tail[a, :, pl.ds(pl.multiple_of(cells + h * BLK, BLK), BLK)]
    rows = partner.point(h, a) * rows
    return spread_tail(rows) if spread else rows


def finish_kernel(steps, level, spread, rim, tail, first_message, rim_out):
    partner = Partner(first_message, steps, level)
    cells = tail.shape[2] - rim.shape[0] * BLK

    def step(h, u):
        for a in range(NV):
            rows = rim_tail(h, a, tail, cells, partner, spread)
            rim_out[h, a] = rim[h, a] - padded(rows, rim.shape[2])

    each_block(rim.shape[0], step)


def rest_part(b, part, rim, table, rim_jacobian):
    lanes = lanes_of(b)
    return rim_part(0, [part[a, :, lanes] for a in range(NV)], b, rim, table, rim_jacobian)


def first_sweep_kernel(weights, table, field, part, tail, rim, rim_jacobian, points, out, *tail_out):
    sweep_kernel(weights, table, field, part, rim, rim_jacobian, points, out, *tail_out)


def sweep_kernel(weights, table, field, part, rim, rim_jacobian, points, out, *tail_out):
    def step(b, u):
        lanes = lanes_of(b)
        total = rest_part(b, part, rim, table, rim_jacobian)
        for a in range(NV):
            out[a, :, lanes] = field[a, :, lanes] + points[pl.ds(a, 1), lanes] * total[a]

    each_block(table.shape[1], step)
    if tail_out:
        send_tail(weights, out, rim, tail_out[0])


def first_correction_kernel(weights, table, part, rim, last_rows, rim_jacobian, points, out, defect_out, *tail_out):
    def step(b, u):
        lanes = lanes_of(b)
        total = rest_part(b, part, rim, table, rim_jacobian)
        for a in range(NV):
            defect_out[a, :, lanes] = total[a]
            out[a, :, lanes] = points[pl.ds(a, 1), lanes] * total[a]

    each_block(table.shape[1], step)
    if tail_out:
        send_tail(weights, out, last_rows, tail_out[0])


def corrected_kernel(weights, table, field, part, rim, fine, rim_jacobian, points, out, *refs):
    scratch = refs[-1]

    def step(b, u):
        lanes = lanes_of(b)
        total = rest_part(b, part, rim, table, rim_jacobian)
        for a in range(NV):
            v = field[a, :, lanes] + points[pl.ds(a, 1), lanes] * total[a]
            out[a, :, lanes] = fine[a, :, lanes] + spread_rows(v, scratch.at[u, a])

    each_block(table.shape[1], step)
    if len(refs) > 1:
        send_tail(weights, out, rim, refs[0])


def last_own_kernel(weight, table, field, goal, jacobian, self_block, cell_diag, out, updated, sem):
    copy = pltpu.make_async_copy(field, updated, sem)
    copy.start()
    own_kernel(weight, table, field, goal, jacobian, self_block, cell_diag, out)
    copy.wait()


def last_rim_kernel(steps, index, faces, message, tail, first_message, out):
    rim_kernel(steps, 0, index, faces, message, first_message, out)
    partner = Partner(first_message, steps, 0)
    cells = tail.shape[2] - index.shape[0] * BLK

    def step(h, u):
        for a in range(NV):
            out[h, a, pl.ds(0, 2), :] = out[h, a, pl.ds(0, 2), :] - rim_tail(h, a, tail, cells, partner, False)

    each_block(index.shape[0], step)


def residual_kernel(table, part, rim, tail, rim_jacobian, out, held, sems):
    blocks = table.shape[1]

    def send(b):
        lanes = lanes_of(b)
        return pltpu.make_async_copy(held.at[:, :, lanes], out.at[:, :, lanes], sems.at[b])

    def step(b, u):
        lanes = lanes_of(b)
        total = rest_part(b, part, rim, table, rim_jacobian)
        for a in range(NV):
            held[a, :, lanes] = total[a]
            add_rows(held, a, lanes, -tail[a, :, lanes])
        send(b).start()

    each_block(blocks, step)
    each_block(blocks, lambda b, u: send(b).wait())


def earlier_steps(b, tail, table, rim_jacobian, partner, spread):
    lanes = lanes_of(b)
    total = [-tail[a, :, lanes] for a in range(NV)]
    if partner is None:
        return total
    if spread:
        total = [padded(rows, 2 * GROUP) for rows in total]
    cells = table.shape[1] * BLK
    block = table[0, b]
    values = [-rim_tail(block, j, tail, cells, partner, spread) for j in range(NV)]
    return coupled(total, lambda a, j: rim_jacobian[0, a, pl.ds(j, 1), lanes], values)


def add_rows(out, a, lanes, rows):
    first = pl.ds(0, rows.shape[0])
    out[a, first, lanes] = out[a, first, lanes] + rows


def partner_of(first_message, steps, level):
    return None if level is None else Partner(first_message, steps, level)


def finish_sweep_kernel(
    steps, level, spread, spread_out, table, listed, field, tail, first_message, rim_jacobian, points, out, faces_out
):
    partner = partner_of(first_message, steps, level)

    def step(b, u):
        lanes = lanes_of(b)
        total = earlier_steps(b, tail, table, rim_jacobian, partner, spread)
        for a in range(NV):
            rows = points[pl.ds(a, 1), lanes] * total[a]
            add_rows(out, a, lanes, spread_tail(rows) if spread_out else rows)

    each_block(table.shape[1], step)
    pick_faces(listed, out, faces_out)


def finish_smoothed_kernel(
    steps, level, table, listed, field, tail, first_message, rim_jacobian, points, out, means_out, faces_out, scratch
):
    partner = partner_of(first_message, steps, level)

    def step(b, u):
        lanes = lanes_of(b)
        total = earlier_steps(b, tail, table, rim_jacobian, partner, False)
        for a in range(NV):
            add_rows(out, a, lanes, points[pl.ds(a, 1), lanes] * total[a])
            means_out[a, :, lanes] = mean_rows(out[a, :, lanes], scratch.at[u, a], means_out.shape[1])

    each_block(table.shape[1], step)
    pick_faces(listed, means_out, faces_out)


def finish_correction_kernel(
    steps, level, table, listed, field, defect, tail, first_message, rim_jacobian, points, out, defect_out, faces_out
):
    partner = partner_of(first_message, steps, level)

    def step(b, u):
        lanes = lanes_of(b)
        total = earlier_steps(b, tail, table, rim_jacobian, partner, False)
        for a in range(NV):
            add_rows(defect_out, a, lanes, total[a])
            add_rows(out, a, lanes, points[pl.ds(a, 1), lanes] * total[a])

    each_block(table.shape[1], step)
    pick_faces(listed, out, faces_out)


def neighbour_pairs(first):
    pairs = [(i, i + 1) for i in range(first, lax.axis_size("space") - 1, 2)]
    return pairs + [(j, i) for i, j in pairs]


def over_chips(message):
    return lax.ppermute(message, "space", neighbour_pairs(1))


def on_chip(faces):
    return lax.ppermute(faces, "space", neighbour_pairs(0))


def to_later(tail):
    periods = lax.axis_size("tm")
    return lax.ppermute(tail, "tm", [(i, (i + 1) % periods) for i in range(periods)])


def body(iterate, right_side, jacobian, self_block, cell_diag, neighbours, face_list):
    steps, cells = iterate.shape[0], iterate.shape[2]
    blocks, faces = cells // BLK, face_list.shape[0]
    coarse = steps // GROUP
    per_slot = 2 * blocks * NV * NV * BLK

    whole = lambda n: shape(NV, n, cells)
    face = lambda n: shape(faces, NV, n, BLK)
    spare = lambda more, n: shape(faces + more, NV, n, BLK)
    rows_scratch = [pltpu.VMEM((UNROLL, NV, steps, BLK), jnp.float32)]
    bind = functools.partial
    plain = lambda rows: rows

    goal = jnp.transpose(right_side, (1, 0, 2))
    jacobian = jnp.transpose(jacobian, (1, 2, 0, 3))
    operands = [jnp.transpose(neighbours), face_list, jnp.transpose(iterate, (1, 0, 2))]
    operands = [in_hbm(x) for x in operands + [cell_diag, jacobian, self_block, goal]]
    table, listed, state, cell_diag, jacobian, self_block, goal, sent = pl.pallas_call(
        first_kernel,
        out_shape=[pltpu.SMEM(x.shape, jnp.int32) for x in operands[:2]]
        + [pltpu.VMEM(x.shape, jnp.float32) for x in [*operands[2:], face(steps)]],
        in_specs=[IN_HBM] * len(operands),
        out_specs=[IN_SMEM] * 2 + [IN_VMEM] * (len(operands) - 1),
        scratch_shapes=[pltpu.SMEM(x.shape, jnp.int32) for x in operands[:2]]
        + [pltpu.SemaphoreType.DMA((len(operands),))],
        compiler_params=pltpu.CompilerParams(vmem_limit_bytes=SCRATCH_BYTES),
        cost_estimate=NOTHING,
        name="arguments",
    )(*operands)
    tables = [table, listed]
    rim = over_chips(sent)
    beside = on_chip(sent)
    fine_points, coarse_points, rim_jacobian = call(
        derived_kernel, "derived", [listed], [cell_diag, jacobian],
        [shape(NV, cells)] * 2 + [shape(2, NV, NV, cells)],
    )

    def own(weight, n, field, target):
        return call(
            bind(own_kernel, weight), "own_part", [table], [field, target, jacobian, self_block, cell_diag],
            [whole(n)], 5 * per_slot * n,
        )[0]

    ahead = coarse >= 4
    tail_shape = shape(NV, 2, cells + faces * BLK)

    first_tail = call(
        bind(tail_kernel, (time_weight, False, None, None)), "tail", [], [state], [shape(NV, 2, 2 * cells)]
    )[0]
    tail = to_later(first_tail)
    part = own(time_weight, steps, state, goal)
    part, message = call(
        first_message_kernel, "first_message", tables,
        [state, part, beside, rim_jacobian, fine_points, coarse_points],
        [whole(steps), shape(faces, NV * steps + NV * (NV + 3), BLK)], per_slot * steps,
    )
    first_message = over_chips(message)
    message = first_message
    earlier_sent = sent

    def plan(weights, tail, level, spread=False):
        def ready(rim):
            if ahead or level is None:
                return rim, level
            return call(
                bind(finish_kernel, steps, level, spread), "finish_rim", [], [rim, tail, first_message],
                [shape(*rim.shape)],
            )[0], None

        return ready

    def sweep(kernel, name, arrays, behind, outs, rim, weights, tail, level, spread, finisher, scratch=(), tail_rim=None):
        rim, level = plan(weights, tail, level, spread)(rim)
        sources = rim if tail_rim is None else tail_rim
        extra = [] if tail_rim is None else [tail_rim]
        results = call(
            bind(kernel, weights), name, [table], arrays + [rim] + extra + behind,
            outs + [tail_shape] * ahead, per_slot * steps, scratch,
        )
        if ahead:
            next_tail = to_later(results[-1])
            results = results[:-1]
        finished = finisher(results, tail, level)
        if not ahead:
            next_tail = to_later(call(bind(tail_kernel, weights), "tail", [], [finished[0], sources], [tail_shape])[0])
        return finished, next_tail, rim

    def finish_with(points, n, spread=False, spread_out=False):
        def finisher(results, tail, level):
            return call(
                bind(finish_sweep_kernel, steps, level, spread, spread_out), "finish_sweep", tables,
                [results[0], tail, points if level is None else first_message, rim_jacobian, points],
                [whole(n), face(n)], 0, (), None, 1,
            )

        return finisher

    fine_weights = (time_weight, False, time_weight, False)
    (state, sent), tail, rim = sweep(
        first_sweep_kernel, "first_sweep", [state, part, tail], [rim_jacobian, fine_points], [whole(steps)], rim, fine_weights,
        tail, None, False, finish_with(fine_points, steps),
    )
    beside = on_chip(sent)
    part = own(time_weight, steps, state, goal)
    part, next_message = call(
        means_message_kernel, "message_of_means", tables, [state, part, beside, rim_jacobian, fine_points],
        [whole(steps), face(coarse + 2)], per_slot * steps, rows_scratch,
    )
    index = pl.pallas_call(
        bind(index_kernel, steps), out_shape=pltpu.SMEM((faces,), jnp.int32), in_specs=[IN_VMEM] * 2,
        out_specs=IN_SMEM, name="coupled_faces", cost_estimate=NOTHING,
        compiler_params=pltpu.CompilerParams(vmem_limit_bytes=SCRATCH_BYTES),
    )(*[pltpu.with_memory_space_constraint(x, pltpu.VMEM) for x in (first_message, next_message)])
    next_message = over_chips(next_message)
    rim = call(
        bind(rim_kernel, steps, 0), "rim", [index], [earlier_sent, message, first_message], [face(steps)],
        per_slot * steps // 2,
    )[0]
    message, earlier_sent = next_message, sent

    def finish_smoothed(results, tail, level):
        return call(
            bind(finish_smoothed_kernel, steps, level), "finish_and_means", tables,
            [results[0], tail, first_message, rim_jacobian, fine_points],
            [whole(steps), whole(coarse), face(coarse)], 0, rows_scratch, None, 1,
        )

    (state, means, sent), tail, rim = sweep(
        sweep_kernel, "sweep", [state, part], [rim_jacobian, fine_points], [whole(steps)], rim,
        (time_weight, True, time_weight, True), tail, 0, False, finish_smoothed,
    )

    beside = on_chip(sent)
    part = call(
        bind(means_kernel, time_weight), "own_part_of_means", [table],
        [state, goal, means, jacobian, self_block, cell_diag], [whole(coarse)], 5 * per_slot * coarse, rows_scratch,
    )[0]
    part, next_message = call(
        scaled_message_kernel, "message_of_correction", tables, [part, beside, rim_jacobian, coarse_points],
        [whole(coarse), spare(faces, coarse)], per_slot * coarse,
    )
    next_message = over_chips(next_message)
    rim, last_rows = call(
        bind(means_rim_kernel, steps), "rim_of_means", [index], [earlier_sent, message, first_message],
        [face(coarse), face(2)], per_slot * steps // 2, rows_scratch,
    )
    message, earlier_sent = next_message, sent

    def finish_correction(results, tail, level):
        return call(
            bind(finish_correction_kernel, steps, level), "finish_correction", tables,
            [*results, tail, first_message, rim_jacobian, coarse_points],
            [whole(coarse), whole(coarse), face(coarse)], 0, (), None, 2,
        )

    (correction, defect, sent), tail, rim = sweep(
        first_correction_kernel, "first_correction", [part], [rim_jacobian, coarse_points],
        [whole(coarse), whole(coarse)], rim, (coarse_weight, False, time_weight, True), tail, 0, False,
        finish_correction, (), last_rows,
    )

    for sweep_no in range(NUC - 1):
        beside = on_chip(sent)
        part = own(coarse_weight, coarse, correction, defect)
        last = sweep_no == NUC - 2
        if last:
            part, next_message = call(
                corrected_message_kernel, "message_of_corrected", tables,
                [correction, part, beside, state, rim_jacobian, coarse_points],
                [whole(coarse), spare(1, steps)], per_slot * coarse, rows_scratch,
            )
        else:
            part, next_message = call(
                message_kernel, "message_of_coarse", tables, [correction, part, beside, rim_jacobian, coarse_points],
                [whole(coarse), spare(faces, coarse)], per_slot * coarse,
            )
        next_message = over_chips(next_message)
        rim = call(
            bind(rim_kernel, steps, 1), "rim_of_coarse", [index], [earlier_sent, message, first_message],
            [face(coarse)], per_slot * coarse // 2,
        )[0]
        message, earlier_sent = next_message, sent
        if last:
            (state, sent), tail, rim = sweep(
                corrected_kernel, "corrected", [correction, part], [state, rim_jacobian, coarse_points],
                [whole(steps)], rim, (time_weight, False, coarse_weight, False), tail, 1, False,
                finish_with(coarse_points, steps, False, True), rows_scratch,
            )
        else:
            (correction, sent), tail, rim = sweep(
                sweep_kernel, "coarse_sweep", [correction, part], [rim_jacobian, coarse_points], [whole(coarse)],
                rim, (coarse_weight, False, coarse_weight, False), tail, 1, False, finish_with(coarse_points, coarse),
            )

    for sweep_no in range(NU2 + 1):
        beside = on_chip(sent)
        if sweep_no == NU2:
            break
        part = own(time_weight, steps, state, goal)
        part, next_message = call(
            message_kernel, "message", tables, [state, part, beside, rim_jacobian, fine_points],
            [whole(steps), spare(1, steps)], per_slot * steps,
        )
        next_message = over_chips(next_message)
        if sweep_no == 0:
            rim = call(
                bind(corrected_rim_kernel, steps), "rim_of_corrected", [index],
                [earlier_sent, message, first_message], [face(steps)], per_slot * coarse // 2, rows_scratch,
            )[0]
        else:
            rim = call(
                bind(rim_kernel, steps, 0), "rim", [index], [earlier_sent, message, first_message],
                [face(steps)], per_slot * steps // 2,
            )[0]
        message, earlier_sent = next_message, sent
        spread = sweep_no == 0
        (state, sent), tail, rim = sweep(
            sweep_kernel, "sweep", [state, part], [rim_jacobian, fine_points], [whole(steps)], rim, fine_weights,
            tail, 1 if spread else 0, spread, finish_with(fine_points, steps, spread),
        )
    part, updated = call(
        bind(last_own_kernel, time_weight), "last_own_part", [table],
        [state, goal, jacobian, self_block, cell_diag], [whole(steps)] * 2, 5 * per_slot * steps,
        [pltpu.SemaphoreType.DMA], [IN_VMEM, IN_HBM],
    )
    part = call(beside_part, "beside_part", [table], [part, beside, rim_jacobian], [whole(steps)], per_slot * steps)[0]
    rim = call(
        bind(last_rim_kernel, steps), "rim", [index], [earlier_sent, message, tail, first_message], [face(steps)],
        per_slot * steps // 2,
    )[0]
    residual = call(
        residual_kernel, "residual", [table], [part, rim, tail, rim_jacobian], [whole(steps)], per_slot * steps,
        [pltpu.VMEM((NV, steps, cells), jnp.float32), pltpu.SemaphoreType.DMA((blocks,))], [IN_HBM],
    )[0]
    return jnp.transpose(updated, (1, 0, 2)), jnp.transpose(residual, (1, 0, 2))


def solution(mesh):
    in_specs = (
        P("tm", None, "space"),
        P("tm", None, "space"),
        P(None, None, None, "space"),
        P(None, None, "space"),
        P(None, "space"),
        P("space", None),
        P("space"),
    )
    out_specs = (P("tm", None, "space"), P("tm", None, "space"))
    return jax.shard_map(body, mesh=mesh, in_specs=in_specs, out_specs=out_specs, check_vma=False)
```

```python
import functools

import jax
import jax.numpy as jnp
from jax import lax
from jax.experimental import pallas as pl
from jax.experimental.pallas import tpu as pltpu
from jax.sharding import PartitionSpec as P

NV = 5
BLK = 128
K = 6
NU1 = 2
NU2 = 2
NUC = 4
GROUP = 4

time_weight = 0.5
coarse_weight = time_weight / GROUP
damping = 0.7

UNROLL = 16
OWN_UNROLL = 8
SCRATCH_BYTES = 4 << 20
IN_VMEM = pl.BlockSpec(memory_space=pltpu.VMEM)
NOTHING = pl.CostEstimate(flops=1, bytes_accessed=1, transcendentals=0)
LONG = pl.CostEstimate(flops=0, bytes_accessed=100 << 20, transcendentals=0)
IN_HBM = pl.BlockSpec(memory_space=pltpu.HBM)
IN_SMEM = pl.BlockSpec(memory_space=pltpu.SMEM)


def call(kernel, name, tables, arrays, outs, flops=0, scratch=(), out_specs=None, in_place=0):
    arrays = [pltpu.with_memory_space_constraint(a, pltpu.VMEM) for a in arrays]
    size = 4 * (sum(a.size for a in arrays) + sum(o.size for o in outs))
    return pl.pallas_call(
        kernel,
        out_shape=[
            o if out_specs and out_specs[i] is IN_HBM else pltpu.VMEM(o.shape, o.dtype) for i, o in enumerate(outs)
        ],
        in_specs=[IN_SMEM] * len(tables) + [IN_VMEM] * len(arrays),
        out_specs=out_specs or [IN_VMEM] * len(outs),
        scratch_shapes=scratch,
        input_output_aliases={len(tables) + i: i for i in range(in_place)},
        cost_estimate=LONG if name.startswith('rim') else NOTHING,
        compiler_params=pltpu.CompilerParams(vmem_limit_bytes=SCRATCH_BYTES),
        name=name,
    )(*tables, *arrays)


def in_hbm(array):
    return pltpu.with_memory_space_constraint(array, pltpu.HBM)


def shape(*dims):
    return jax.ShapeDtypeStruct(dims, jnp.float32)


def lanes_of(b):
    return pl.ds(pl.multiple_of(b * BLK, BLK), BLK)


def cross_slot():
    return lax.rem(lax.axis_index("space"), 2)


def each_block(count, step, unroll=UNROLL):
    unroll = min(unroll, count) if count % min(unroll, count) == 0 else 1

    def steps(i, carry):
        for u in range(unroll):
            step(i * unroll + u, u)
        return carry

    lax.fori_loop(0, count // unroll, steps, 0)


def first_kernel(*refs):
    sources, (table, listed, *held, faces_out, near, named, sems) = refs[:7], refs[7:]
    copies = [pltpu.make_async_copy(x, y, sems.at[i]) for i, (x, y) in enumerate(zip(sources, [near, named, *held]))]
    for copy in copies:
        copy.start()
    slot = cross_slot()
    slots, blocks = near.shape
    faces = named.shape[0]
    copies[0].wait()

    def step(b, carry):
        table[0, b] = near[slot, b] - (blocks + faces * slot)
        table[1, b] = near[1 - slot, b] - (blocks + faces * (1 - slot))
        for k in range(2, slots):
            table[k, b] = near[k, b]
        return carry

    lax.fori_loop(0, blocks, step, 0)
    copies[1].wait()
    for h in range(faces):
        listed[h] = named[h]
    copies[2].wait()
    pick_faces(listed, held[0], faces_out)
    for copy in copies[3:]:
        copy.wait()


def derived_kernel(listed, cell_diag, jacobian, fine_out, coarse_out, out):
    lower_crosses = cross_slot() == 0
    fine_out[...] = damping / (3.0 * time_weight + cell_diag[...])
    coarse_out[...] = damping / (3.0 * coarse_weight + cell_diag[...])
    for a in range(NV):
        for j in range(NV):
            lower, upper = jacobian[a, j, pl.ds(0, 1), :], jacobian[a, j, pl.ds(1, 1), :]
            out[0, a, pl.ds(j, 1), :] = jnp.where(lower_crosses, lower, upper)
            out[1, a, pl.ds(j, 1), :] = jnp.where(lower_crosses, upper, lower)


def coupled(total, coupling, values):
    for j in range(NV):
        for a in range(NV):
            total[a] = total[a] - coupling(a, j) * values[j]
    return total


def earlier(v, steps):
    if v.shape[0] <= steps:
        return jnp.zeros_like(v)
    return jnp.concatenate([jnp.zeros((steps, BLK), jnp.float32), v[: v.shape[0] - steps]], axis=0)


def own_part(total, b, field, table, jacobian, self_block):
    lanes = lanes_of(b)
    v = [field[j, :, lanes] for j in range(NV)]
    for a in range(NV):
        for j in range(NV):
            if j != a:
                total[a] = total[a] - self_block[a, pl.ds(j, 1), lanes] * v[j]
    for slot in range(2, K):
        there = lanes_of(table[slot, b])
        row = pl.ds(slot, 1)
        total = coupled(total, lambda a, j: jacobian[a, j, row, lanes], [field[j, :, there] for j in range(NV)])
    return total


def rim_part(side, total, b, rim, table, rim_jacobian):
    block, lanes = table[side, b], lanes_of(b)
    coupling = lambda a, j: rim_jacobian[side, a, pl.ds(j, 1), lanes]
    return coupled(total, coupling, [rim[block, j] for j in range(NV)])


def pick_faces(listed, field, faces_out):
    for h in range(listed.shape[0]):
        lanes = lanes_of(listed[h])
        for a in range(NV):
            faces_out[h, a] = field[a, :, lanes]


def tail_rows(last_two, weight, mean):
    last = last_two[1:]
    if mean:
        return jnp.concatenate([(weight / GROUP) * (last_two[:1] - 3.0 * last), jnp.zeros_like(last)], axis=0)
    return weight * jnp.concatenate([last_two[:1] - 4.0 * last, last], axis=0)


def send_tail(weights, field, rim, tail_out):
    steps, cells = field.shape[1:]
    weight, mean, rim_weight, rim_mean = weights
    for a in range(NV):
        before, last = field[a, pl.ds(steps - 2, 1), :], field[a, pl.ds(steps - 1, 1), :]
        if mean:
            tail_out[a, pl.ds(0, 1), pl.ds(0, cells)] = (weight / GROUP) * (before - 3.0 * last)
            tail_out[a, pl.ds(1, 1), pl.ds(0, cells)] = jnp.zeros_like(last)
        else:
            tail_out[a, pl.ds(0, 1), pl.ds(0, cells)] = weight * (before - 4.0 * last)
            tail_out[a, pl.ds(1, 1), pl.ds(0, cells)] = weight * last
    if rim is not None:
        for h in range(rim.shape[0]):
            for a in range(NV):
                rows = tail_rows(rim[h, a, pl.ds(rim.shape[2] - 2, 2), :], rim_weight, rim_mean)
                tail_out[a, :, pl.ds(cells + h * BLK, BLK)] = rows


def tail_kernel(weights, field, *refs):
    send_tail(weights, field, refs[0] if len(refs) > 1 else None, refs[-1])


def own_kernel(weight, table, field, goal, jacobian, self_block, cell_diag, out):
    def step(b, u):
        lanes = lanes_of(b)
        total = []
        for a in range(NV):
            v = field[a, :, lanes]
            point = 3.0 * weight + cell_diag[pl.ds(a, 1), lanes]
            timed = weight * (earlier(v, 2) - 4.0 * earlier(v, 1))
            total.append(goal[a, :, lanes] - point * v - timed)
        total = own_part(total, b, field, table, jacobian, self_block)
        for a in range(NV):
            out[a, :, lanes] = total[a]

    each_block(table.shape[1], step, OWN_UNROLL)


def mean_rows(v, scratch, steps):
    scratch[...] = v
    return sum(scratch[pl.ds(i, steps, stride=GROUP), :] for i in range(GROUP)) * (1.0 / GROUP)


def spread_rows(v, scratch):
    for i in range(GROUP):
        scratch[pl.ds(i, v.shape[0], stride=GROUP), :] = v
    return scratch[...]


def means_kernel(weight, table, field, goal, means, jacobian, self_block, cell_diag, out, scratch):
    steps = means.shape[1]

    def step(b, u):
        lanes = lanes_of(b)
        total = []
        for a in range(NV):
            v = field[a, :, lanes]
            fine = goal[a, :, lanes] - weight * (3.0 * v - 4.0 * earlier(v, 1) + earlier(v, 2))
            total.append(mean_rows(fine, scratch.at[u, a], steps) - cell_diag[pl.ds(a, 1), lanes] * means[a, :, lanes])
        total = own_part(total, b, means, table, jacobian, self_block)
        for a in range(NV):
            out[a, :, lanes] = total[a]

    each_block(table.shape[1], step, OWN_UNROLL)


def beside_part(table, part, rim, rim_jacobian, out):
    def step(b, u):
        lanes = lanes_of(b)
        total = rim_part(1, [part[a, :, lanes] for a in range(NV)], b, rim, table, rim_jacobian)
        for a in range(NV):
            out[a, :, lanes] = total[a]

    each_block(table.shape[1], step)


def step_of(listed, h, a, field, part, points):
    lanes = lanes_of(listed[h])
    return field[a, :, lanes] + points[pl.ds(a, 1), lanes] * part[a, :, lanes]


def message_kernel(table, listed, field, part, rim, rim_jacobian, points, out, message):
    beside_part(table, part, rim, rim_jacobian, out)
    for h in range(listed.shape[0]):
        for a in range(NV):
            message[h, a] = step_of(listed, h, a, field, out, points)


def first_message_kernel(
    table, listed, field, part, rim, rim_jacobian, points, coarse_points, out, message
):
    beside_part(table, part, rim, rim_jacobian, out)
    steps = field.shape[1]
    behind = NV * steps
    for h in range(listed.shape[0]):
        block = listed[h]
        lanes = lanes_of(block)
        for a in range(NV):
            message[h, pl.ds(a * steps, steps), :] = step_of(listed, h, a, field, out, points)
            message[h, pl.ds(behind + NV * a, NV), :] = rim_jacobian[0, a, :, lanes]
        message[h, pl.ds(behind + NV * NV, NV), :] = points[:, lanes]
        message[h, pl.ds(behind + NV * NV + NV, NV), :] = coarse_points[:, lanes]
        named = jnp.full((1, BLK), table[0, block], jnp.int32)
        message[h, pl.ds(behind + NV * NV + 2 * NV, 1), :] = named.astype(jnp.float32)


def means_message_kernel(table, listed, field, part, rim, rim_jacobian, points, out, message, scratch):
    beside_part(table, part, rim, rim_jacobian, out)
    steps = field.shape[1]
    coarse = steps // GROUP
    for h in range(listed.shape[0]):
        for a in range(NV):
            v = step_of(listed, h, a, field, out, points)
            message[h, a, pl.ds(0, coarse), :] = mean_rows(v, scratch.at[h % UNROLL, a], coarse)
            message[h, a, pl.ds(coarse, 2), :] = v[steps - 2 :]


def scaled_message_kernel(table, listed, part, rim, rim_jacobian, points, out, message):
    beside_part(table, part, rim, rim_jacobian, out)
    for h in range(listed.shape[0]):
        lanes = lanes_of(listed[h])
        for a in range(NV):
            message[h, a] = points[pl.ds(a, 1), lanes] * out[a, :, lanes]


def corrected_message_kernel(table, listed, field, part, rim, fine, rim_jacobian, points, out, message, scratch):
    beside_part(table, part, rim, rim_jacobian, out)
    for h in range(listed.shape[0]):
        for a in range(NV):
            v = step_of(listed, h, a, field, out, points)
            message[h, a] = fine[a, :, lanes_of(listed[h])] + spread_rows(v, scratch.at[h % UNROLL, a])


class Partner:
    def __init__(self, ref, steps, level):
        self.ref, self.behind, self.level = ref, NV * steps, level

    def row(self, h, r):
        return self.ref[h, pl.ds(self.behind + r, 1), :]

    def coupling(self, h):
        return lambda a, j: self.row(h, NV * a + j)

    def point(self, h, a):
        return self.row(h, NV * (NV + self.level) + a)


def index_kernel(steps, message, next_message, index):
    partner = Partner(message, steps, 0)
    for h in range(index.shape[0]):
        index[h] = jnp.max(partner.row(h, NV * (NV + 2))).astype(jnp.int32)


def own_share(index, h, faces, partner):
    block = index[h]
    zero = [jnp.zeros(faces.shape[2:], jnp.float32)] * NV
    total = coupled(zero, partner.coupling(h), [faces[block, j] for j in range(NV)])
    return [partner.point(h, a) * total[a] for a in range(NV)]


def rim_kernel(steps, level, index, faces, message, first_message, out):
    partner = Partner(first_message, steps, level)

    def step(h, u):
        share = own_share(index, h, faces, partner)
        for a in range(NV):
            if len(message.shape) == 3:
                out[h, a] = message[h, pl.ds(a * steps, steps), :] + share[a]
            else:
                out[h, a] = message[h, a] + share[a]

    each_block(index.shape[0], step)


def means_rim_kernel(steps, index, faces, message, first_message, out, last_out, scratch):
    partner = Partner(first_message, steps, 0)
    coarse = out.shape[2]

    def step(h, u):
        share = own_share(index, h, faces, partner)
        for a in range(NV):
            out[h, a] = message[h, a, pl.ds(0, coarse), :] + mean_rows(share[a], scratch.at[u, a], coarse)
            last_out[h, a] = message[h, a, pl.ds(coarse, 2), :] + share[a][steps - 2 :]

    each_block(index.shape[0], step)


def corrected_rim_kernel(steps, index, faces, message, first_message, out, scratch):
    partner = Partner(first_message, steps, 1)

    def step(h, u):
        share = own_share(index, h, faces, partner)
        for a in range(NV):
            out[h, a] = message[h, a] + spread_rows(share[a], scratch.at[u, a])

    each_block(index.shape[0], step)


def padded(rows, count):
    pad = count - rows.shape[0]
    return jnp.concatenate([rows, jnp.zeros((pad, BLK), jnp.float32)], axis=0) if pad > 0 else rows


def spread_tail(rows):
    return jnp.concatenate([jnp.broadcast_to(rows[i : i + 1], (GROUP, BLK)) for i in range(2)], axis=0)


def rim_tail(h, a, tail, cells, partner, spread):
    rows = tail[a, :, pl.ds(pl.multiple_of(cells + h * BLK, BLK), BLK)]
    rows = partner.point(h, a) * rows
    return spread_tail(rows) if spread else rows


def finish_kernel(steps, cells, level, spread, rim, tail, first_message, rim_out):
    partner = Partner(first_message, steps, level)

    def step(h, u):
        for a in range(NV):
            rows = rim_tail(h, a, tail, cells, partner, spread)
            rim_out[h, a] = rim[h, a] - padded(rows, rim.shape[2])

    each_block(rim.shape[0], step)


def rest_part(b, part, rim, table, rim_jacobian):
    lanes = lanes_of(b)
    return rim_part(0, [part[a, :, lanes] for a in range(NV)], b, rim, table, rim_jacobian)


def first_sweep_kernel(weights, table, field, part, tail, rim, rim_jacobian, points, out, *tail_out):
    sweep_kernel(weights, table, field, part, rim, rim_jacobian, points, out, *tail_out)


def sweep_kernel(weights, table, field, part, rim, rim_jacobian, points, out, *tail_out):
    def step(b, u):
        lanes = lanes_of(b)
        total = rest_part(b, part, rim, table, rim_jacobian)
        for a in range(NV):
            out[a, :, lanes] = field[a, :, lanes] + points[pl.ds(a, 1), lanes] * total[a]

    each_block(table.shape[1], step)
    if tail_out:
        send_tail(weights, out, rim, tail_out[0])


def first_correction_kernel(weights, table, part, rim, last_rows, rim_jacobian, points, out, defect_out, *tail_out):
    def step(b, u):
        lanes = lanes_of(b)
        total = rest_part(b, part, rim, table, rim_jacobian)
        for a in range(NV):
            defect_out[a, :, lanes] = total[a]
            out[a, :, lanes] = points[pl.ds(a, 1), lanes] * total[a]

    each_block(table.shape[1], step)
    if tail_out:
        send_tail(weights, out, last_rows, tail_out[0])


def corrected_kernel(weights, table, field, part, rim, fine, rim_jacobian, points, out, *refs):
    scratch = refs[-1]

    def step(b, u):
        lanes = lanes_of(b)
        total = rest_part(b, part, rim, table, rim_jacobian)
        for a in range(NV):
            v = field[a, :, lanes] + points[pl.ds(a, 1), lanes] * total[a]
            out[a, :, lanes] = fine[a, :, lanes] + spread_rows(v, scratch.at[u, a])

    each_block(table.shape[1], step)
    if len(refs) > 1:
        send_tail(weights, out, rim, refs[0])


def last_own_kernel(weight, table, field, goal, jacobian, self_block, cell_diag, out, updated, sem):
    copy = pltpu.make_async_copy(field, updated, sem)
    copy.start()
    own_kernel(weight, table, field, goal, jacobian, self_block, cell_diag, out)
    copy.wait()


def last_rim_kernel(steps, cells, index, faces, message, tail, first_message, out):
    rim_kernel(steps, 0, index, faces, message, first_message, out)
    partner = Partner(first_message, steps, 0)

    def step(h, u):
        for a in range(NV):
            out[h, a, pl.ds(0, 2), :] = out[h, a, pl.ds(0, 2), :] - rim_tail(h, a, tail, cells, partner, False)

    each_block(index.shape[0], step)


def residual_kernel(table, part, rim, tail, rim_jacobian, out, held, sems):
    blocks = table.shape[1]

    def send(b):
        lanes = lanes_of(b)
        return pltpu.make_async_copy(held.at[:, :, lanes], out.at[:, :, lanes], sems.at[b])

    def step(b, u):
        lanes = lanes_of(b)
        total = rest_part(b, part, rim, table, rim_jacobian)
        for a in range(NV):
            held[a, :, lanes] = total[a]
            add_rows(held, a, lanes, -tail[a, :, lanes])
        send(b).start()

    each_block(blocks, step)
    each_block(blocks, lambda b, u: send(b).wait())


def earlier_steps(b, tail, table, rim_jacobian, partner, spread):
    lanes = lanes_of(b)
    total = [-tail[a, :, lanes] for a in range(NV)]
    if partner is None:
        return total
    if spread:
        total = [padded(rows, 2 * GROUP) for rows in total]
    cells = table.shape[1] * BLK
    block = table[0, b]
    values = [-rim_tail(block, j, tail, cells, partner, spread) for j in range(NV)]
    return coupled(total, lambda a, j: rim_jacobian[0, a, pl.ds(j, 1), lanes], values)


def add_rows(out, a, lanes, rows):
    first = pl.ds(0, rows.shape[0])
    out[a, first, lanes] = out[a, first, lanes] + rows


def partner_of(first_message, steps, level):
    return None if level is None else Partner(first_message, steps, level)


def finish_sweep_kernel(
    steps, level, spread, spread_out, table, listed, field, tail, first_message, rim_jacobian, points, out, faces_out
):
    partner = partner_of(first_message, steps, level)

    def step(b, u):
        lanes = lanes_of(b)
        total = earlier_steps(b, tail, table, rim_jacobian, partner, spread)
        for a in range(NV):
            rows = points[pl.ds(a, 1), lanes] * total[a]
            add_rows(out, a, lanes, spread_tail(rows) if spread_out else rows)

    each_block(table.shape[1], step)
    pick_faces(listed, out, faces_out)


def finish_smoothed_kernel(
    steps, level, table, listed, field, tail, first_message, rim_jacobian, points, out, means_out, faces_out, scratch
):
    partner = partner_of(first_message, steps, level)

    def step(b, u):
        lanes = lanes_of(b)
        total = earlier_steps(b, tail, table, rim_jacobian, partner, False)
        for a in range(NV):
            add_rows(out, a, lanes, points[pl.ds(a, 1), lanes] * total[a])
            means_out[a, :, lanes] = mean_rows(out[a, :, lanes], scratch.at[u, a], means_out.shape[1])

    each_block(table.shape[1], step)
    pick_faces(listed, means_out, faces_out)


def finish_correction_kernel(
    steps, level, table, listed, field, defect, tail, first_message, rim_jacobian, points, out, defect_out, faces_out
):
    partner = partner_of(first_message, steps, level)

    def step(b, u):
        lanes = lanes_of(b)
        total = earlier_steps(b, tail, table, rim_jacobian, partner, False)
        for a in range(NV):
            add_rows(defect_out, a, lanes, total[a])
            add_rows(out, a, lanes, points[pl.ds(a, 1), lanes] * total[a])

    each_block(table.shape[1], step)
    pick_faces(listed, out, faces_out)


def neighbour_pairs(first):
    pairs = [(i, i + 1) for i in range(first, lax.axis_size("space") - 1, 2)]
    return pairs + [(j, i) for i, j in pairs]


def over_chips(message):
    return lax.ppermute(message, "space", neighbour_pairs(1))


def on_chip(faces):
    return lax.ppermute(faces, "space", neighbour_pairs(0))


def to_later(tail):
    periods = lax.axis_size("tm")
    return lax.ppermute(tail, "tm", [(i, (i + 1) % periods) for i in range(periods)])


def body(iterate, right_side, jacobian, self_block, cell_diag, neighbours, face_list):
    steps, cells = iterate.shape[0], iterate.shape[2]
    blocks, faces = cells // BLK, face_list.shape[0]
    coarse = steps // GROUP
    per_slot = 2 * blocks * NV * NV * BLK

    whole = lambda n: shape(NV, n, cells)
    face = lambda n: shape(faces, NV, n, BLK)
    spare = lambda more, n: shape(faces + more, NV, n, BLK)
    rows_scratch = [pltpu.VMEM((UNROLL, NV, steps, BLK), jnp.float32)]
    bind = functools.partial
    plain = lambda rows: rows

    goal = jnp.transpose(right_side, (1, 0, 2))
    jacobian = jnp.transpose(jacobian, (1, 2, 0, 3))
    operands = [jnp.transpose(neighbours), face_list, jnp.transpose(iterate, (1, 0, 2))]
    operands = [in_hbm(x) for x in operands + [cell_diag, jacobian, self_block, goal]]
    table, listed, state, cell_diag, jacobian, self_block, goal, sent = pl.pallas_call(
        first_kernel,
        out_shape=[pltpu.SMEM(x.shape, jnp.int32) for x in operands[:2]]
        + [pltpu.VMEM(x.shape, jnp.float32) for x in [*operands[2:], face(steps)]],
        in_specs=[IN_HBM] * len(operands),
        out_specs=[IN_SMEM] * 2 + [IN_VMEM] * (len(operands) - 1),
        scratch_shapes=[pltpu.SMEM(x.shape, jnp.int32) for x in operands[:2]]
        + [pltpu.SemaphoreType.DMA((len(operands),))],
        compiler_params=pltpu.CompilerParams(vmem_limit_bytes=SCRATCH_BYTES),
        cost_estimate=NOTHING,
        name="arguments",
    )(*operands)
    tables = [table, listed]
    rim = over_chips(sent)
    beside = on_chip(sent)
    fine_points, coarse_points, rim_jacobian = call(
        derived_kernel, "derived", [listed], [cell_diag, jacobian],
        [shape(NV, cells)] * 2 + [shape(2, NV, NV, cells)],
    )

    def own(weight, n, field, target):
        return call(
            bind(own_kernel, weight), "own_part", [table], [field, target, jacobian, self_block, cell_diag],
            [whole(n)], 5 * per_slot * n,
        )[0]

    ahead = coarse >= 4
    tail_shape = shape(NV, 2, cells + faces * BLK)

    first_tail = call(
        bind(tail_kernel, (time_weight, False, None, None)), "tail", [], [state], [shape(NV, 2, 2 * cells)]
    )[0]
    tail = to_later(first_tail)
    part = own(time_weight, steps, state, goal)
    part, message = call(
        first_message_kernel, "first_message", tables,
        [state, part, beside, rim_jacobian, fine_points, coarse_points],
        [whole(steps), shape(faces, NV * steps + NV * (NV + 3), BLK)], per_slot * steps,
    )
    first_message = over_chips(message)
    message = first_message
    earlier_sent = sent

    def plan(weights, tail, level, spread=False):
        def ready(rim):
            if ahead or level is None:
                return rim, level
            return call(
                bind(finish_kernel, steps, cells, level, spread), "finish_rim", [], [rim, tail, first_message],
                [shape(*rim.shape)],
            )[0], None

        return ready

    def sweep(kernel, name, arrays, behind, outs, rim, weights, tail, level, spread, finisher, scratch=(), tail_rim=None):
        rim, level = plan(weights, tail, level, spread)(rim)
        sources = rim if tail_rim is None else tail_rim
        extra = [] if tail_rim is None else [tail_rim]
        results = call(
            bind(kernel, weights), name, [table], arrays + [rim] + extra + behind,
            outs + [tail_shape] * ahead, per_slot * steps, scratch,
        )
        if ahead:
            next_tail = to_later(results[-1])
            results = results[:-1]
        finished = finisher(results, tail, level)
        if not ahead:
            next_tail = to_later(call(bind(tail_kernel, weights), "tail", [], [finished[0], sources], [tail_shape])[0])
        return finished, next_tail, rim

    def finish_with(points, n, spread=False, spread_out=False):
        def finisher(results, tail, level):
            return call(
                bind(finish_sweep_kernel, steps, level, spread, spread_out), "finish_sweep", tables,
                [results[0], tail, points if level is None else first_message, rim_jacobian, points],
                [whole(n), face(n)], 0, (), None, 1,
            )

        return finisher

    fine_weights = (time_weight, False, time_weight, False)
    (state, sent), tail, rim = sweep(
        first_sweep_kernel, "first_sweep", [state, part, tail], [rim_jacobian, fine_points], [whole(steps)], rim, fine_weights,
        tail, None, False, finish_with(fine_points, steps),
    )
    beside = on_chip(sent)
    part = own(time_weight, steps, state, goal)
    part, next_message = call(
        means_message_kernel, "message_of_means", tables, [state, part, beside, rim_jacobian, fine_points],
        [whole(steps), face(coarse + 2)], per_slot * steps, rows_scratch,
    )
    index = pl.pallas_call(
        bind(index_kernel, steps), out_shape=pltpu.SMEM((faces,), jnp.int32), in_specs=[IN_VMEM] * 2,
        out_specs=IN_SMEM, name="coupled_faces", cost_estimate=NOTHING,
        compiler_params=pltpu.CompilerParams(vmem_limit_bytes=SCRATCH_BYTES),
    )(*[pltpu.with_memory_space_constraint(x, pltpu.VMEM) for x in (first_message, next_message)])
    next_message = over_chips(next_message)
    rim = call(
        bind(rim_kernel, steps, 0), "rim", [index], [earlier_sent, message, first_message], [face(steps)],
        per_slot * steps // 2,
    )[0]
    message, earlier_sent = next_message, sent

    def finish_smoothed(results, tail, level):
        return call(
            bind(finish_smoothed_kernel, steps, level), "finish_and_means", tables,
            [results[0], tail, first_message, rim_jacobian, fine_points],
            [whole(steps), whole(coarse), face(coarse)], 0, rows_scratch, None, 1,
        )

    (state, means, sent), tail, rim = sweep(
        sweep_kernel, "sweep", [state, part], [rim_jacobian, fine_points], [whole(steps)], rim,
        (time_weight, True, time_weight, True), tail, 0, False, finish_smoothed,
    )

    beside = on_chip(sent)
    part = call(
        bind(means_kernel, time_weight), "own_part_of_means", [table],
        [state, goal, means, jacobian, self_block, cell_diag], [whole(coarse)], 5 * per_slot * coarse, rows_scratch,
    )[0]
    part, next_message = call(
        scaled_message_kernel, "message_of_correction", tables, [part, beside, rim_jacobian, coarse_points],
        [whole(coarse), spare(faces, coarse)], per_slot * coarse,
    )
    next_message = over_chips(next_message)
    rim, last_rows = call(
        bind(means_rim_kernel, steps), "rim_of_means", [index], [earlier_sent, message, first_message],
        [face(coarse), face(2)], per_slot * steps // 2, rows_scratch,
    )
    message, earlier_sent = next_message, sent

    def finish_correction(results, tail, level):
        return call(
            bind(finish_correction_kernel, steps, level), "finish_correction", tables,
            [*results, tail, first_message, rim_jacobian, coarse_points],
            [whole(coarse), whole(coarse), face(coarse)], 0, (), None, 2,
        )

    (correction, defect, sent), tail, rim = sweep(
        first_correction_kernel, "first_correction", [part], [rim_jacobian, coarse_points],
        [whole(coarse), whole(coarse)], rim, (coarse_weight, False, time_weight, True), tail, 0, False,
        finish_correction, (), last_rows,
    )

    for sweep_no in range(NUC - 1):
        beside = on_chip(sent)
        part = own(coarse_weight, coarse, correction, defect)
        last = sweep_no == NUC - 2
        if last:
            part, next_message = call(
                corrected_message_kernel, "message_of_corrected", tables,
                [correction, part, beside, state, rim_jacobian, coarse_points],
                [whole(coarse), spare(1, steps)], per_slot * coarse, rows_scratch,
            )
        else:
            part, next_message = call(
                message_kernel, "message_of_coarse", tables, [correction, part, beside, rim_jacobian, coarse_points],
                [whole(coarse), spare(faces, coarse)], per_slot * coarse,
            )
        next_message = over_chips(next_message)
        rim = call(
            bind(rim_kernel, steps, 1), "rim_of_coarse", [index], [earlier_sent, message, first_message],
            [face(coarse)], per_slot * coarse // 2,
        )[0]
        message, earlier_sent = next_message, sent
        if last:
            (state, sent), tail, rim = sweep(
                corrected_kernel, "corrected", [correction, part], [state, rim_jacobian, coarse_points],
                [whole(steps)], rim, (time_weight, False, coarse_weight, False), tail, 1, False,
                finish_with(coarse_points, steps, False, True), rows_scratch,
            )
        else:
            (correction, sent), tail, rim = sweep(
                sweep_kernel, "coarse_sweep", [correction, part], [rim_jacobian, coarse_points], [whole(coarse)],
                rim, (coarse_weight, False, coarse_weight, False), tail, 1, False, finish_with(coarse_points, coarse),
            )

    for sweep_no in range(NU2 + 1):
        beside = on_chip(sent)
        if sweep_no == NU2:
            break
        part = own(time_weight, steps, state, goal)
        part, next_message = call(
            message_kernel, "message", tables, [state, part, beside, rim_jacobian, fine_points],
            [whole(steps), spare(1, steps)], per_slot * steps,
        )
        next_message = over_chips(next_message)
        if sweep_no == 0:
            rim = call(
                bind(corrected_rim_kernel, steps), "rim_of_corrected", [index],
                [earlier_sent, message, first_message], [face(steps)], per_slot * coarse // 2, rows_scratch,
            )[0]
        else:
            rim = call(
                bind(rim_kernel, steps, 0), "rim", [index], [earlier_sent, message, first_message],
                [face(steps)], per_slot * steps // 2,
            )[0]
        message, earlier_sent = next_message, sent
        spread = sweep_no == 0
        (state, sent), tail, rim = sweep(
            sweep_kernel, "sweep", [state, part], [rim_jacobian, fine_points], [whole(steps)], rim, fine_weights,
            tail, 1 if spread else 0, spread, finish_with(fine_points, steps, spread),
        )
    part, updated = call(
        bind(last_own_kernel, time_weight), "last_own_part", [table],
        [state, goal, jacobian, self_block, cell_diag], [whole(steps)] * 2, 5 * per_slot * steps,
        [pltpu.SemaphoreType.DMA], [IN_VMEM, IN_HBM],
    )
    part = call(beside_part, "beside_part", [table], [part, beside, rim_jacobian], [whole(steps)], per_slot * steps)[0]
    rim = call(
        bind(last_rim_kernel, steps, cells), "rim", [index], [earlier_sent, message, tail, first_message], [face(steps)],
        per_slot * steps // 2,
    )[0]
    residual = call(
        residual_kernel, "residual", [table], [part, rim, tail, rim_jacobian], [whole(steps)], per_slot * steps,
        [pltpu.VMEM((NV, steps, cells), jnp.float32), pltpu.SemaphoreType.DMA((blocks,))], [IN_HBM],
    )[0]
    return jnp.transpose(updated, (1, 0, 2)), jnp.transpose(residual, (1, 0, 2))


def solution(mesh):
    in_specs = (
        P("tm", None, "space"),
        P("tm", None, "space"),
        P(None, None, None, "space"),
        P(None, None, "space"),
        P(None, "space"),
        P("space", None),
        P("space"),
    )
    out_specs = (P("tm", None, "space"), P("tm", None, "space"))
    return jax.shard_map(body, mesh=mesh, in_specs=in_specs, out_specs=out_specs, check_vma=False)
```

```python
import functools

import jax
import jax.numpy as jnp
from jax import lax
from jax.experimental import pallas as pl
from jax.experimental.pallas import tpu as pltpu
from jax.sharding import PartitionSpec as P

NV = 5
BLK = 128
K = 6
NU1 = 2
NU2 = 2
NUC = 4
GROUP = 4

time_weight = 0.5
coarse_weight = time_weight / GROUP
damping = 0.7

UNROLL = 16
OWN_UNROLL = 8
SCRATCH_BYTES = 4 << 20
IN_VMEM = pl.BlockSpec(memory_space=pltpu.VMEM)
NOTHING = pl.CostEstimate(flops=1, bytes_accessed=1, transcendentals=0)
LONG = pl.CostEstimate(flops=0, bytes_accessed=100 << 20, transcendentals=0)
IN_HBM = pl.BlockSpec(memory_space=pltpu.HBM)
IN_SMEM = pl.BlockSpec(memory_space=pltpu.SMEM)


def call(kernel, name, tables, arrays, outs, flops=0, scratch=(), out_specs=None, in_place=0):
    arrays = [pltpu.with_memory_space_constraint(a, pltpu.VMEM) for a in arrays]
    size = 4 * (sum(a.size for a in arrays) + sum(o.size for o in outs))
    return pl.pallas_call(
        kernel,
        out_shape=[
            o if out_specs and out_specs[i] is IN_HBM else pltpu.VMEM(o.shape, o.dtype) for i, o in enumerate(outs)
        ],
        in_specs=[IN_SMEM] * len(tables) + [IN_VMEM] * len(arrays),
        out_specs=out_specs or [IN_VMEM] * len(outs),
        scratch_shapes=scratch,
        input_output_aliases={len(tables) + i: i for i in range(in_place)},
        cost_estimate=LONG if name.startswith('rim') else NOTHING,
        compiler_params=pltpu.CompilerParams(vmem_limit_bytes=SCRATCH_BYTES),
        name=name,
    )(*tables, *arrays)


def in_hbm(array):
    return pltpu.with_memory_space_constraint(array, pltpu.HBM)


def shape(*dims):
    return jax.ShapeDtypeStruct(dims, jnp.float32)


def lanes_of(b):
    return pl.ds(pl.multiple_of(b * BLK, BLK), BLK)


def cross_slot():
    return lax.rem(lax.axis_index("space"), 2)


def each_block(count, step, unroll=UNROLL):
    unroll = min(unroll, count) if count % min(unroll, count) == 0 else 1

    def steps(i, carry):
        for u in range(unroll):
            step(i * unroll + u, u)
        return carry

    lax.fori_loop(0, count // unroll, steps, 0)


def first_kernel(*refs):
    sources, (table, listed, *held, faces_out, near, named, sems) = refs[:7], refs[7:]
    copies = [pltpu.make_async_copy(x, y, sems.at[i]) for i, (x, y) in enumerate(zip(sources, [near, named, *held]))]
    for copy in copies:
        copy.start()
    slot = cross_slot()
    slots, blocks = near.shape
    faces = named.shape[0]
    copies[0].wait()

    def step(b, carry):
        table[0, b] = near[slot, b] - (blocks + faces * slot)
        table[1, b] = near[1 - slot, b] - (blocks + faces * (1 - slot))
        for k in range(2, slots):
            table[k, b] = near[k, b]
        return carry

    lax.fori_loop(0, blocks, step, 0)
    copies[1].wait()
    for h in range(faces):
        listed[h] = named[h]
    copies[2].wait()
    pick_faces(listed, held[0], faces_out)
    for copy in copies[3:]:
        copy.wait()


def derived_kernel(listed, cell_diag, jacobian, fine_out, coarse_out, out):
    lower_crosses = cross_slot() == 0
    fine_out[...] = damping / (3.0 * time_weight + cell_diag[...])
    coarse_out[...] = damping / (3.0 * coarse_weight + cell_diag[...])
    for a in range(NV):
        for j in range(NV):
            lower, upper = jacobian[a, j, pl.ds(0, 1), :], jacobian[a, j, pl.ds(1, 1), :]
            out[0, a, pl.ds(j, 1), :] = jnp.where(lower_crosses, lower, upper)
            out[1, a, pl.ds(j, 1), :] = jnp.where(lower_crosses, upper, lower)


def coupled(total, coupling, values):
    for j in range(NV):
        for a in range(NV):
            total[a] = total[a] - coupling(a, j) * values[j]
    return total


def earlier(v, steps):
    if v.shape[0] <= steps:
        return jnp.zeros_like(v)
    return jnp.concatenate([jnp.zeros((steps, BLK), jnp.float32), v[: v.shape[0] - steps]], axis=0)


def own_part(total, b, field, table, jacobian, self_block):
    lanes = lanes_of(b)
    v = [field[j, :, lanes] for j in range(NV)]
    for a in range(NV):
        for j in range(NV):
            if j != a:
                total[a] = total[a] - self_block[a, pl.ds(j, 1), lanes] * v[j]
    for slot in range(2, K):
        there = lanes_of(table[slot, b])
        row = pl.ds(slot, 1)
        total = coupled(total, lambda a, j: jacobian[a, j, row, lanes], [field[j, :, there] for j in range(NV)])
    return total


def rim_part(side, total, b, rim, table, rim_jacobian):
    block, lanes = table[side, b], lanes_of(b)
    coupling = lambda a, j: rim_jacobian[side, a, pl.ds(j, 1), lanes]
    return coupled(total, coupling, [rim[block, j] for j in range(NV)])


def pick_faces(listed, field, faces_out):
    for h in range(listed.shape[0]):
        lanes = lanes_of(listed[h])
        for a in range(NV):
            faces_out[h, a] = field[a, :, lanes]


def tail_rows(last_two, weight, mean):
    last = last_two[1:]
    if mean:
        return jnp.concatenate([(weight / GROUP) * (last_two[:1] - 3.0 * last), jnp.zeros_like(last)], axis=0)
    return weight * jnp.concatenate([last_two[:1] - 4.0 * last, last], axis=0)


def send_tail(weights, field, rim, tail_out):
    steps, cells = field.shape[1:]
    weight, mean, rim_weight, rim_mean = weights
    for a in range(NV):
        before, last = field[a, pl.ds(steps - 2, 1), :], field[a, pl.ds(steps - 1, 1), :]
        if mean:
            tail_out[a, pl.ds(0, 1), pl.ds(0, cells)] = (weight / GROUP) * (before - 3.0 * last)
            tail_out[a, pl.ds(1, 1), pl.ds(0, cells)] = jnp.zeros_like(last)
        else:
            tail_out[a, pl.ds(0, 1), pl.ds(0, cells)] = weight * (before - 4.0 * last)
            tail_out[a, pl.ds(1, 1), pl.ds(0, cells)] = weight * last
    if rim is not None:
        for h in range(rim.shape[0]):
            for a in range(NV):
                rows = tail_rows(rim[h, a, pl.ds(rim.shape[2] - 2, 2), :], rim_weight, rim_mean)
                tail_out[a, :, pl.ds(cells + h * BLK, BLK)] = rows


def tail_kernel(weights, field, *refs):
    send_tail(weights, field, refs[0] if len(refs) > 1 else None, refs[-1])


def own_kernel(weight, table, field, goal, jacobian, self_block, cell_diag, out):
    def step(b, u):
        lanes = lanes_of(b)
        total = []
        for a in range(NV):
            v = field[a, :, lanes]
            point = 3.0 * weight + cell_diag[pl.ds(a, 1), lanes]
            timed = weight * (earlier(v, 2) - 4.0 * earlier(v, 1))
            total.append(goal[a, :, lanes] - point * v - timed)
        total = own_part(total, b, field, table, jacobian, self_block)
        for a in range(NV):
            out[a, :, lanes] = total[a]

    each_block(table.shape[1], step, OWN_UNROLL)


def mean_rows(v, scratch, steps):
    scratch[...] = v
    return sum(scratch[pl.ds(i, steps, stride=GROUP), :] for i in range(GROUP)) * (1.0 / GROUP)


def spread_rows(v, scratch):
    for i in range(GROUP):
        scratch[pl.ds(i, v.shape[0], stride=GROUP), :] = v
    return scratch[...]


def means_kernel(weight, table, field, goal, means, jacobian, self_block, cell_diag, out, scratch):
    steps = means.shape[1]

    def step(b, u):
        lanes = lanes_of(b)
        total = []
        for a in range(NV):
            held = scratch.at[u + OWN_UNROLL, a]
            held[...] = field[a, :, lanes]
            before, last = (held[pl.ds(i, steps, stride=GROUP), :] for i in (GROUP - 2, GROUP - 1))
            timed = 3.0 * (last - earlier(last, 1)) - (before - earlier(before, 1))
            fixed = mean_rows(goal[a, :, lanes], scratch.at[u, a], steps) - (weight / GROUP) * timed
            total.append(fixed - cell_diag[pl.ds(a, 1), lanes] * means[a, :, lanes])
        total = own_part(total, b, means, table, jacobian, self_block)
        for a in range(NV):
            out[a, :, lanes] = total[a]

    each_block(table.shape[1], step, OWN_UNROLL)


def beside_part(table, part, rim, rim_jacobian, out):
    def step(b, u):
        lanes = lanes_of(b)
        total = rim_part(1, [part[a, :, lanes] for a in range(NV)], b, rim, table, rim_jacobian)
        for a in range(NV):
            out[a, :, lanes] = total[a]

    each_block(table.shape[1], step)


def step_of(listed, h, a, field, part, points):
    lanes = lanes_of(listed[h])
    return field[a, :, lanes] + points[pl.ds(a, 1), lanes] * part[a, :, lanes]


def message_kernel(table, listed, field, part, rim, rim_jacobian, points, out, message):
    beside_part(table, part, rim, rim_jacobian, out)
    for h in range(listed.shape[0]):
        for a in range(NV):
            message[h, a] = step_of(listed, h, a, field, out, points)


def first_message_kernel(
    table, listed, field, part, rim, rim_jacobian, points, coarse_points, out, message
):
    beside_part(table, part, rim, rim_jacobian, out)
    steps = field.shape[1]
    behind = NV * steps
    for h in range(listed.shape[0]):
        block = listed[h]
        lanes = lanes_of(block)
        for a in range(NV):
            message[h, pl.ds(a * steps, steps), :] = step_of(listed, h, a, field, out, points)
            message[h, pl.ds(behind + NV * a, NV), :] = rim_jacobian[0, a, :, lanes]
        message[h, pl.ds(behind + NV * NV, NV), :] = points[:, lanes]
        message[h, pl.ds(behind + NV * NV + NV, NV), :] = coarse_points[:, lanes]
        named = jnp.full((1, BLK), table[0, block], jnp.int32)
        message[h, pl.ds(behind + NV * NV + 2 * NV, 1), :] = named.astype(jnp.float32)


def means_message_kernel(table, listed, field, part, rim, rim_jacobian, points, out, message, scratch):
    beside_part(table, part, rim, rim_jacobian, out)
    steps = field.shape[1]
    coarse = steps // GROUP
    for h in range(listed.shape[0]):
        for a in range(NV):
            v = step_of(listed, h, a, field, out, points)
            message[h, a, pl.ds(0, coarse), :] = mean_rows(v, scratch.at[h % UNROLL, a], coarse)
            message[h, a, pl.ds(coarse, 2), :] = v[steps - 2 :]


def scaled_message_kernel(table, listed, part, rim, rim_jacobian, points, out, message):
    beside_part(table, part, rim, rim_jacobian, out)
    for h in range(listed.shape[0]):
        lanes = lanes_of(listed[h])
        for a in range(NV):
            message[h, a] = points[pl.ds(a, 1), lanes] * out[a, :, lanes]


def corrected_message_kernel(table, listed, field, part, rim, fine, rim_jacobian, points, out, message, scratch):
    beside_part(table, part, rim, rim_jacobian, out)
    for h in range(listed.shape[0]):
        for a in range(NV):
            v = step_of(listed, h, a, field, out, points)
            message[h, a] = fine[a, :, lanes_of(listed[h])] + spread_rows(v, scratch.at[h % UNROLL, a])


class Partner:
    def __init__(self, ref, steps, level):
        self.ref, self.behind, self.level = ref, NV * steps, level

    def row(self, h, r):
        return self.ref[h, pl.ds(self.behind + r, 1), :]

    def coupling(self, h):
        return lambda a, j: self.row(h, NV * a + j)

    def point(self, h, a):
        return self.row(h, NV * (NV + self.level) + a)


def index_kernel(steps, message, next_message, index):
    partner = Partner(message, steps, 0)
    for h in range(index.shape[0]):
        index[h] = jnp.max(partner.row(h, NV * (NV + 2))).astype(jnp.int32)


def own_share(index, h, faces, partner):
    block = index[h]
    zero = [jnp.zeros(faces.shape[2:], jnp.float32)] * NV
    total = coupled(zero, partner.coupling(h), [faces[block, j] for j in range(NV)])
    return [partner.point(h, a) * total[a] for a in range(NV)]


def rim_kernel(steps, level, index, faces, message, first_message, out):
    partner = Partner(first_message, steps, level)

    def step(h, u):
        share = own_share(index, h, faces, partner)
        for a in range(NV):
            if len(message.shape) == 3:
                out[h, a] = message[h, pl.ds(a * steps, steps), :] + share[a]
            else:
                out[h, a] = message[h, a] + share[a]

    each_block(index.shape[0], step)


def means_rim_kernel(steps, index, faces, message, first_message, out, last_out, scratch):
    partner = Partner(first_message, steps, 0)
    coarse = out.shape[2]

    def step(h, u):
        share = own_share(index, h, faces, partner)
        for a in range(NV):
            out[h, a] = message[h, a, pl.ds(0, coarse), :] + mean_rows(share[a], scratch.at[u, a], coarse)
            last_out[h, a] = message[h, a, pl.ds(coarse, 2), :] + share[a][steps - 2 :]

    each_block(index.shape[0], step)


def corrected_rim_kernel(steps, index, faces, message, first_message, out, scratch):
    partner = Partner(first_message, steps, 1)

    def step(h, u):
        share = own_share(index, h, faces, partner)
        for a in range(NV):
            out[h, a] = message[h, a] + spread_rows(share[a], scratch.at[u, a])

    each_block(index.shape[0], step)


def padded(rows, count):
    pad = count - rows.shape[0]
    return jnp.concatenate([rows, jnp.zeros((pad, BLK), jnp.float32)], axis=0) if pad > 0 else rows


def spread_tail(rows):
    return jnp.concatenate([jnp.broadcast_to(rows[i : i + 1], (GROUP, BLK)) for i in range(2)], axis=0)


def rim_tail(h, a, tail, cells, partner, spread):
    rows = tail[a, :, pl.ds(pl.multiple_of(cells + h * BLK, BLK), BLK)]
    rows = partner.point(h, a) * rows
    return spread_tail(rows) if spread else rows


def finish_kernel(steps, cells, level, spread, rim, tail, first_message, rim_out):
    partner = Partner(first_message, steps, level)

    def step(h, u):
        for a in range(NV):
            rows = rim_tail(h, a, tail, cells, partner, spread)
            rim_out[h, a] = rim[h, a] - padded(rows, rim.shape[2])

    each_block(rim.shape[0], step)


def rest_part(b, part, rim, table, rim_jacobian):
    lanes = lanes_of(b)
    return rim_part(0, [part[a, :, lanes] for a in range(NV)], b, rim, table, rim_jacobian)


def first_sweep_kernel(weights, table, field, part, tail, rim, rim_jacobian, points, out, *tail_out):
    sweep_kernel(weights, table, field, part, rim, rim_jacobian, points, out, *tail_out)


def sweep_kernel(weights, table, field, part, rim, rim_jacobian, points, out, *tail_out):
    def step(b, u):
        lanes = lanes_of(b)
        total = rest_part(b, part, rim, table, rim_jacobian)
        for a in range(NV):
            out[a, :, lanes] = field[a, :, lanes] + points[pl.ds(a, 1), lanes] * total[a]

    each_block(table.shape[1], step)
    if tail_out:
        send_tail(weights, out, rim, tail_out[0])


def first_correction_kernel(weights, table, part, rim, last_rows, rim_jacobian, points, out, defect_out, *tail_out):
    def step(b, u):
        lanes = lanes_of(b)
        total = rest_part(b, part, rim, table, rim_jacobian)
        for a in range(NV):
            defect_out[a, :, lanes] = total[a]
            out[a, :, lanes] = points[pl.ds(a, 1), lanes] * total[a]

    each_block(table.shape[1], step)
    if tail_out:
        send_tail(weights, out, last_rows, tail_out[0])


def corrected_kernel(weights, table, field, part, rim, fine, rim_jacobian, points, out, *refs):
    scratch = refs[-1]

    def step(b, u):
        lanes = lanes_of(b)
        total = rest_part(b, part, rim, table, rim_jacobian)
        for a in range(NV):
            v = field[a, :, lanes] + points[pl.ds(a, 1), lanes] * total[a]
            out[a, :, lanes] = fine[a, :, lanes] + spread_rows(v, scratch.at[u, a])

    each_block(table.shape[1], step)
    if len(refs) > 1:
        send_tail(weights, out, rim, refs[0])


def last_own_kernel(weight, table, field, goal, jacobian, self_block, cell_diag, out, updated, sem):
    copy = pltpu.make_async_copy(field, updated, sem)
    copy.start()
    own_kernel(weight, table, field, goal, jacobian, self_block, cell_diag, out)
    copy.wait()


def last_rim_kernel(steps, cells, index, faces, message, tail, first_message, out):
    rim_kernel(steps, 0, index, faces, message, first_message, out)
    partner = Partner(first_message, steps, 0)

    def step(h, u):
        for a in range(NV):
            out[h, a, pl.ds(0, 2), :] = out[h, a, pl.ds(0, 2), :] - rim_tail(h, a, tail, cells, partner, False)

    each_block(index.shape[0], step)


def residual_kernel(table, part, rim, tail, rim_jacobian, out, held, sems):
    blocks = table.shape[1]

    def send(b):
        lanes = lanes_of(b)
        return pltpu.make_async_copy(held.at[:, :, lanes], out.at[:, :, lanes], sems.at[b])

    def step(b, u):
        lanes = lanes_of(b)
        total = rest_part(b, part, rim, table, rim_jacobian)
        for a in range(NV):
            held[a, :, lanes] = total[a]
            add_rows(held, a, lanes, -tail[a, :, lanes])
        send(b).start()

    each_block(blocks, step)
    each_block(blocks, lambda b, u: send(b).wait())


def earlier_steps(b, tail, table, rim_jacobian, partner, spread):
    lanes = lanes_of(b)
    total = [-tail[a, :, lanes] for a in range(NV)]
    if partner is None:
        return total
    if spread:
        total = [padded(rows, 2 * GROUP) for rows in total]
    cells = table.shape[1] * BLK
    block = table[0, b]
    values = [-rim_tail(block, j, tail, cells, partner, spread) for j in range(NV)]
    return coupled(total, lambda a, j: rim_jacobian[0, a, pl.ds(j, 1), lanes], values)


def add_rows(out, a, lanes, rows):
    first = pl.ds(0, rows.shape[0])
    out[a, first, lanes] = out[a, first, lanes] + rows


def partner_of(first_message, steps, level):
    return None if level is None else Partner(first_message, steps, level)


def finish_sweep_kernel(
    steps, level, spread, spread_out, table, listed, field, tail, first_message, rim_jacobian, points, out, faces_out
):
    partner = partner_of(first_message, steps, level)

    def step(b, u):
        lanes = lanes_of(b)
        total = earlier_steps(b, tail, table, rim_jacobian, partner, spread)
        for a in range(NV):
            rows = points[pl.ds(a, 1), lanes] * total[a]
            add_rows(out, a, lanes, spread_tail(rows) if spread_out else rows)

    each_block(table.shape[1], step)
    pick_faces(listed, out, faces_out)


def finish_smoothed_kernel(
    steps, level, table, listed, field, tail, first_message, rim_jacobian, points, out, means_out, faces_out, scratch
):
    partner = partner_of(first_message, steps, level)

    def step(b, u):
        lanes = lanes_of(b)
        total = earlier_steps(b, tail, table, rim_jacobian, partner, False)
        for a in range(NV):
            add_rows(out, a, lanes, points[pl.ds(a, 1), lanes] * total[a])
            means_out[a, :, lanes] = mean_rows(out[a, :, lanes], scratch.at[u, a], means_out.shape[1])

    each_block(table.shape[1], step)
    pick_faces(listed, means_out, faces_out)


def finish_correction_kernel(
    steps, level, table, listed, field, defect, tail, first_message, rim_jacobian, points, out, defect_out, faces_out
):
    partner = partner_of(first_message, steps, level)

    def step(b, u):
        lanes = lanes_of(b)
        total = earlier_steps(b, tail, table, rim_jacobian, partner, False)
        for a in range(NV):
            add_rows(defect_out, a, lanes, total[a])
            add_rows(out, a, lanes, points[pl.ds(a, 1), lanes] * total[a])

    each_block(table.shape[1], step)
    pick_faces(listed, out, faces_out)


def neighbour_pairs(first):
    pairs = [(i, i + 1) for i in range(first, lax.axis_size("space") - 1, 2)]
    return pairs + [(j, i) for i, j in pairs]


def over_chips(message):
    return lax.ppermute(message, "space", neighbour_pairs(1))


def on_chip(faces):
    return lax.ppermute(faces, "space", neighbour_pairs(0))


def to_later(tail):
    periods = lax.axis_size("tm")
    return lax.ppermute(tail, "tm", [(i, (i + 1) % periods) for i in range(periods)])


def body(iterate, right_side, jacobian, self_block, cell_diag, neighbours, face_list):
    steps, cells = iterate.shape[0], iterate.shape[2]
    blocks, faces = cells // BLK, face_list.shape[0]
    coarse = steps // GROUP
    per_slot = 2 * blocks * NV * NV * BLK

    whole = lambda n: shape(NV, n, cells)
    face = lambda n: shape(faces, NV, n, BLK)
    spare = lambda more, n: shape(faces + more, NV, n, BLK)
    rows_scratch = [pltpu.VMEM((UNROLL, NV, steps, BLK), jnp.float32)]
    bind = functools.partial
    plain = lambda rows: rows

    goal = jnp.transpose(right_side, (1, 0, 2))
    jacobian = jnp.transpose(jacobian, (1, 2, 0, 3))
    operands = [jnp.transpose(neighbours), face_list, jnp.transpose(iterate, (1, 0, 2))]
    operands = [in_hbm(x) for x in operands + [cell_diag, jacobian, self_block, goal]]
    table, listed, state, cell_diag, jacobian, self_block, goal, sent = pl.pallas_call(
        first_kernel,
        out_shape=[pltpu.SMEM(x.shape, jnp.int32) for x in operands[:2]]
        + [pltpu.VMEM(x.shape, jnp.float32) for x in [*operands[2:], face(steps)]],
        in_specs=[IN_HBM] * len(operands),
        out_specs=[IN_SMEM] * 2 + [IN_VMEM] * (len(operands) - 1),
        scratch_shapes=[pltpu.SMEM(x.shape, jnp.int32) for x in operands[:2]]
        + [pltpu.SemaphoreType.DMA((len(operands),))],
        compiler_params=pltpu.CompilerParams(vmem_limit_bytes=SCRATCH_BYTES),
        cost_estimate=NOTHING,
        name="arguments",
    )(*operands)
    tables = [table, listed]
    rim = over_chips(sent)
    beside = on_chip(sent)
    fine_points, coarse_points, rim_jacobian = call(
        derived_kernel, "derived", [listed], [cell_diag, jacobian],
        [shape(NV, cells)] * 2 + [shape(2, NV, NV, cells)],
    )

    def own(weight, n, field, target):
        return call(
            bind(own_kernel, weight), "own_part", [table], [field, target, jacobian, self_block, cell_diag],
            [whole(n)], 5 * per_slot * n,
        )[0]

    ahead = coarse >= 4
    tail_shape = shape(NV, 2, cells + faces * BLK)

    first_tail = call(
        bind(tail_kernel, (time_weight, False, None, None)), "tail", [], [state], [shape(NV, 2, 2 * cells)]
    )[0]
    tail = to_later(first_tail)
    part = own(time_weight, steps, state, goal)
    part, message = call(
        first_message_kernel, "first_message", tables,
        [state, part, beside, rim_jacobian, fine_points, coarse_points],
        [whole(steps), shape(faces, NV * steps + NV * (NV + 3), BLK)], per_slot * steps,
    )
    first_message = over_chips(message)
    message = first_message
    earlier_sent = sent

    def plan(weights, tail, level, spread=False):
        def ready(rim):
            if ahead or level is None:
                return rim, level
            return call(
                bind(finish_kernel, steps, cells, level, spread), "finish_rim", [], [rim, tail, first_message],
                [shape(*rim.shape)],
            )[0], None

        return ready

    def sweep(kernel, name, arrays, behind, outs, rim, weights, tail, level, spread, finisher, scratch=(), tail_rim=None):
        rim, level = plan(weights, tail, level, spread)(rim)
        sources = rim if tail_rim is None else tail_rim
        extra = [] if tail_rim is None else [tail_rim]
        results = call(
            bind(kernel, weights), name, [table], arrays + [rim] + extra + behind,
            outs + [tail_shape] * ahead, per_slot * steps, scratch,
        )
        if ahead:
            next_tail = to_later(results[-1])
            results = results[:-1]
        finished = finisher(results, tail, level)
        if not ahead:
            next_tail = to_later(call(bind(tail_kernel, weights), "tail", [], [finished[0], sources], [tail_shape])[0])
        return finished, next_tail, rim

    def finish_with(points, n, spread=False, spread_out=False):
        def finisher(results, tail, level):
            return call(
                bind(finish_sweep_kernel, steps, level, spread, spread_out), "finish_sweep", tables,
                [results[0], tail, points if level is None else first_message, rim_jacobian, points],
                [whole(n), face(n)], 0, (), None, 1,
            )

        return finisher

    fine_weights = (time_weight, False, time_weight, False)
    (state, sent), tail, rim = sweep(
        first_sweep_kernel, "first_sweep", [state, part, tail], [rim_jacobian, fine_points], [whole(steps)], rim, fine_weights,
        tail, None, False, finish_with(fine_points, steps),
    )
    beside = on_chip(sent)
    part = own(time_weight, steps, state, goal)
    part, next_message = call(
        means_message_kernel, "message_of_means", tables, [state, part, beside, rim_jacobian, fine_points],
        [whole(steps), face(coarse + 2)], per_slot * steps, rows_scratch,
    )
    index = pl.pallas_call(
        bind(index_kernel, steps), out_shape=pltpu.SMEM((faces,), jnp.int32), in_specs=[IN_VMEM] * 2,
        out_specs=IN_SMEM, name="coupled_faces", cost_estimate=NOTHING,
        compiler_params=pltpu.CompilerParams(vmem_limit_bytes=SCRATCH_BYTES),
    )(*[pltpu.with_memory_space_constraint(x, pltpu.VMEM) for x in (first_message, next_message)])
    next_message = over_chips(next_message)
    rim = call(
        bind(rim_kernel, steps, 0), "rim", [index], [earlier_sent, message, first_message], [face(steps)],
        per_slot * steps // 2,
    )[0]
    message, earlier_sent = next_message, sent

    def finish_smoothed(results, tail, level):
        return call(
            bind(finish_smoothed_kernel, steps, level), "finish_and_means", tables,
            [results[0], tail, first_message, rim_jacobian, fine_points],
            [whole(steps), whole(coarse), face(coarse)], 0, rows_scratch, None, 1,
        )

    (state, means, sent), tail, rim = sweep(
        sweep_kernel, "sweep", [state, part], [rim_jacobian, fine_points], [whole(steps)], rim,
        (time_weight, True, time_weight, True), tail, 0, False, finish_smoothed,
    )

    beside = on_chip(sent)
    part = call(
        bind(means_kernel, time_weight), "own_part_of_means", [table],
        [state, goal, means, jacobian, self_block, cell_diag], [whole(coarse)], 5 * per_slot * coarse, rows_scratch,
    )[0]
    part, next_message = call(
        scaled_message_kernel, "message_of_correction", tables, [part, beside, rim_jacobian, coarse_points],
        [whole(coarse), spare(faces, coarse)], per_slot * coarse,
    )
    next_message = over_chips(next_message)
    rim, last_rows = call(
        bind(means_rim_kernel, steps), "rim_of_means", [index], [earlier_sent, message, first_message],
        [face(coarse), face(2)], per_slot * steps // 2, rows_scratch,
    )
    message, earlier_sent = next_message, sent

    def finish_correction(results, tail, level):
        return call(
            bind(finish_correction_kernel, steps, level), "finish_correction", tables,
            [*results, tail, first_message, rim_jacobian, coarse_points],
            [whole(coarse), whole(coarse), face(coarse)], 0, (), None, 2,
        )

    (correction, defect, sent), tail, rim = sweep(
        first_correction_kernel, "first_correction", [part], [rim_jacobian, coarse_points],
        [whole(coarse), whole(coarse)], rim, (coarse_weight, False, time_weight, True), tail, 0, False,
        finish_correction, (), last_rows,
    )

    for sweep_no in range(NUC - 1):
        beside = on_chip(sent)
        part = own(coarse_weight, coarse, correction, defect)
        last = sweep_no == NUC - 2
        if last:
            part, next_message = call(
                corrected_message_kernel, "message_of_corrected", tables,
                [correction, part, beside, state, rim_jacobian, coarse_points],
                [whole(coarse), spare(1, steps)], per_slot * coarse, rows_scratch,
            )
        else:
            part, next_message = call(
                message_kernel, "message_of_coarse", tables, [correction, part, beside, rim_jacobian, coarse_points],
                [whole(coarse), spare(faces, coarse)], per_slot * coarse,
            )
        next_message = over_chips(next_message)
        rim = call(
            bind(rim_kernel, steps, 1), "rim_of_coarse", [index], [earlier_sent, message, first_message],
            [face(coarse)], per_slot * coarse // 2,
        )[0]
        message, earlier_sent = next_message, sent
        if last:
            (state, sent), tail, rim = sweep(
                corrected_kernel, "corrected", [correction, part], [state, rim_jacobian, coarse_points],
                [whole(steps)], rim, (time_weight, False, coarse_weight, False), tail, 1, False,
                finish_with(coarse_points, steps, False, True), rows_scratch,
            )
        else:
            (correction, sent), tail, rim = sweep(
                sweep_kernel, "coarse_sweep", [correction, part], [rim_jacobian, coarse_points], [whole(coarse)],
                rim, (coarse_weight, False, coarse_weight, False), tail, 1, False, finish_with(coarse_points, coarse),
            )

    for sweep_no in range(NU2 + 1):
        beside = on_chip(sent)
        if sweep_no == NU2:
            break
        part = own(time_weight, steps, state, goal)
        part, next_message = call(
            message_kernel, "message", tables, [state, part, beside, rim_jacobian, fine_points],
            [whole(steps), spare(1, steps)], per_slot * steps,
        )
        next_message = over_chips(next_message)
        if sweep_no == 0:
            rim = call(
                bind(corrected_rim_kernel, steps), "rim_of_corrected", [index],
                [earlier_sent, message, first_message], [face(steps)], per_slot * coarse // 2, rows_scratch,
            )[0]
        else:
            rim = call(
                bind(rim_kernel, steps, 0), "rim", [index], [earlier_sent, message, first_message],
                [face(steps)], per_slot * steps // 2,
            )[0]
        message, earlier_sent = next_message, sent
        spread = sweep_no == 0
        (state, sent), tail, rim = sweep(
            sweep_kernel, "sweep", [state, part], [rim_jacobian, fine_points], [whole(steps)], rim, fine_weights,
            tail, 1 if spread else 0, spread, finish_with(fine_points, steps, spread),
        )
    part, updated = call(
        bind(last_own_kernel, time_weight), "last_own_part", [table],
        [state, goal, jacobian, self_block, cell_diag], [whole(steps)] * 2, 5 * per_slot * steps,
        [pltpu.SemaphoreType.DMA], [IN_VMEM, IN_HBM],
    )
    part = call(beside_part, "beside_part", [table], [part, beside, rim_jacobian], [whole(steps)], per_slot * steps)[0]
    rim = call(
        bind(last_rim_kernel, steps, cells), "rim", [index], [earlier_sent, message, tail, first_message], [face(steps)],
        per_slot * steps // 2,
    )[0]
    residual = call(
        residual_kernel, "residual", [table], [part, rim, tail, rim_jacobian], [whole(steps)], per_slot * steps,
        [pltpu.VMEM((NV, steps, cells), jnp.float32), pltpu.SemaphoreType.DMA((blocks,))], [IN_HBM],
    )[0]
    return jnp.transpose(updated, (1, 0, 2)), jnp.transpose(residual, (1, 0, 2))


def solution(mesh):
    in_specs = (
        P("tm", None, "space"),
        P("tm", None, "space"),
        P(None, None, None, "space"),
        P(None, None, "space"),
        P(None, "space"),
        P("space", None),
        P("space"),
    )
    out_specs = (P("tm", None, "space"), P("tm", None, "space"))
    return jax.shard_map(body, mesh=mesh, in_specs=in_specs, out_specs=out_specs, check_vma=False)
```
